128 devices in a mesh: sub: 16 (over y, x), grp: 8 (over z, core).
Axes of the slice: x: 4, y: 4, z: 4, core: 2. Of those that a mesh axis runs over, the one named last changes fastest.
Arguments:
- schur: bfloat16 [128, 2560, 2560], P(('sub', 'grp'))
- coarse_basis: float32 [128, 6, 2560], P(('sub', 'grp')), may hold values from -0.125 to 0.125
- coarse_inverse: float32 [768, 768], P(('sub', 'grp'))
- coarse_coeff: float32 [128, 6, 96], P(('sub', 'grp')), may hold values from -160 to 160
- dual_load: float32 [128, 96, 2560], P(('sub', 'grp'))
- face_order: int32 [128, 2, 512], P(('sub', 'grp')), may hold values from 0 to 511, each once within a row
- contact_partner: int32 [128, 256], P(('sub', 'grp')), may hold values from 0 to 255, as said below
- active_flags: int32 [128, 96, 256], P(('sub', 'grp')), may hold values from 0 to 1, as said below
- step_codes: int32 [96, 3], replicated, may hold values from 0 to 2
Outputs:
- multipliers: float32 [128, 96, 2560], P(('sub', 'grp'))
- gradient: float32 [128, 96, 2560], P(('sub', 'grp'))
The draws below stay inside these ranges and needn't reach their ends.
Inputs may be any that keep to these rules, and one draw needn't show every extreme that they name: `contact_partner`: the subdomains at (i, j) and (i, j + 4) hold mutually inverse maps. `active_flags`: the two multipliers of a contact pair carry the same flag.
All inputs are finite; a program needn't handle non-finite values.
Results may differ from the reference program's by a relative error of at most 0.0035.
Values sent between devices are 32-bit elements; how exact they have to be, the bound alone decides.
No kernel may reach another device: no remote copies, remote signals or barrier semaphores. Data moves between devices by JAX's collectives and lax.ppermute only.
A program may use at most 128 MiB of HBM per device.

```python
import jax
import jax.numpy as jnp
from jax import lax

FACE = 512
CONT = 256
DIRI = 256
ORDER = 2560
MODES = 6
NLOAD = 96
ITERS = 3
SUBS = 16
GROUPS = 8
DOMAINS = 128
NCOARSE = 768


def draw_schur(key, part):
    key = jax.random.fold_in(key, 3)
    spread = 0.35 / ORDER ** 0.5

    def draw_block(domain_index):
        block_key = jax.random.fold_in(key, domain_index)
        first_key, second_key = jax.random.split(block_key)
        growth = 1.0 + 2.0 * domain_index.astype(jnp.float32) / max(DOMAINS - 1, 1)
        entries = jax.random.normal(first_key, (ORDER, ORDER), jnp.float32)
        diagonal = jnp.exp(jax.random.uniform(second_key, (ORDER,), jnp.float32, 0.0, 0.6931))
        symmetric = (entries + entries.T) * 0.5 ** 0.5 * spread
        return (growth * (symmetric + jnp.diag(diagonal))).astype(jnp.bfloat16)
    return lax.map(draw_block, jnp.arange(DOMAINS))


def draw_coarse_inverse(key, part):
    key = jax.random.fold_in(key, 5)
    first_key, second_key = jax.random.split(key)
    spread = 0.5 / NCOARSE ** 0.5
    entries = jax.random.normal(first_key, (NCOARSE, NCOARSE), jnp.float32)
    diagonal = jax.random.uniform(second_key, (NCOARSE,), jnp.float32, 1.2, 1.6)
    return (entries + entries.T) * 0.5 ** 0.5 * spread + jnp.diag(diagonal)


def draw_dual_load(key, part):
    key = jax.random.fold_in(key, 7)
    first_key = jax.random.fold_in(key, 0)
    growth = 1.0 + 2.0 * jnp.arange(DOMAINS, dtype=jnp.float32) / max(DOMAINS - 1, 1)
    entries = jax.random.normal(first_key, (DOMAINS, NLOAD, ORDER), jnp.float32)
    return entries * growth[:, None, None]


def pair_maps(key):
    half_groups = GROUPS // 2

    def draw_map(pair_index):
        return jax.random.permutation(jax.random.fold_in(key, pair_index), CONT)
    first_maps = jax.vmap(draw_map)(jnp.arange(SUBS * half_groups)).astype(jnp.int32)
    second_maps = jnp.argsort(first_maps, axis=1).astype(jnp.int32)
    first_maps = first_maps.reshape(SUBS, half_groups, CONT)
    second_maps = second_maps.reshape(SUBS, half_groups, CONT)
    return (first_maps, second_maps)


def draw_contact_partner(key, part):
    first_maps, second_maps = pair_maps(jax.random.fold_in(key, 11))
    return jnp.concatenate([first_maps, second_maps], axis=1).reshape(DOMAINS, CONT).astype(jnp.int32)


def draw_active_flags(key, part):
    half_groups = GROUPS // 2
    first_maps, second_maps = pair_maps(jax.random.fold_in(key, 11))
    base_flags = jax.random.randint(jax.random.fold_in(key, 23), (SUBS, half_groups, NLOAD, CONT), 0, 2).astype(jnp.int32)
    index_map = jnp.broadcast_to(second_maps[:, :, None, :], base_flags.shape)
    partner_flags = jnp.take_along_axis(base_flags, index_map, axis=3)
    return jnp.concatenate([base_flags, partner_flags], axis=1).reshape(DOMAINS, NLOAD, CONT).astype(jnp.int32)


def touch_ends(values, own_key, least, high):
    longest = values.shape.index(max(values.shape))
    spots = []
    for shift in (0, 1):
        where = [jax.random.randint(jax.random.fold_in(own_key, axis), (), 0, length) for axis, length in enumerate(values.shape)]
        where[longest] = (where[longest] + shift) % values.shape[longest]
        spots.append(tuple(where))
    return values.at[spots[0]].set(least).at[spots[1]].set(high)


def level_of(key, dims, cuts, low, largest):
    factor_of, own = 1.0, jax.random.fold_in(key, 6)
    for position, shards_of in cuts:
        draws = jnp.exp(jax.random.uniform(jax.random.fold_in(own, position), (shards_of,), jnp.float32, low / len(cuts), largest / len(cuts)))
        factor_of = factor_of * jnp.repeat(draws, dims[position] // shards_of).reshape([-1 if axis == position else 1 for axis in range(len(dims))])
    return factor_of


def centred(rng, shape, width, reach, cuts=(), kind=jnp.bfloat16):
    loudness = level_of(rng, shape, cuts, -0.22, 0.18) if cuts else 1.0
    result = jax.random.normal(rng, shape, jnp.float32) * width * loudness
    return jnp.minimum(jnp.maximum(result, -reach), reach).astype(kind)


def setup_inputs(seed: int = 0) -> dict:
    key_list = jax.random.split(jax.random.key(seed), 10)
    schur = draw_schur(jax.random.fold_in(key_list[9], 71), 0)
    coarse_basis = centred(key_list[1], (DOMAINS, MODES, ORDER), ORDER ** -0.5, 0.125, ((0, 128),), jnp.float32)
    coarse_inverse = draw_coarse_inverse(jax.random.fold_in(key_list[9], 71), 0)
    coarse_coeff = centred(key_list[3], (DOMAINS, MODES, NLOAD), (0.5 * ORDER ** 0.5), 160.0, ((0, 128),), jnp.float32)
    dual_load = draw_dual_load(jax.random.fold_in(key_list[9], 71), 0)
    face_order = jax.vmap(lambda own: jax.random.permutation(own, FACE))(jax.random.split(key_list[5], DOMAINS * 2)).reshape((DOMAINS, 2, FACE)).astype(jnp.int32)
    contact_partner = draw_contact_partner(jax.random.fold_in(key_list[9], 71), 0)
    active_flags = draw_active_flags(jax.random.fold_in(key_list[9], 71), 0)
    step_codes = touch_ends(jax.random.randint(key_list[8], (NLOAD, ITERS), 0, 3), jax.random.fold_in(key_list[8], 1), 0, 2).astype(jnp.int32)
    return {"schur": schur, "coarse_basis": coarse_basis, "coarse_inverse": coarse_inverse, "coarse_coeff": coarse_coeff, "dual_load": dual_load, "face_order": face_order, "contact_partner": contact_partner, "active_flags": active_flags, "step_codes": step_codes}


highest = lax.Precision.HIGHEST
step_scale = 0.2


def face_flags():
    sub_index = jnp.arange(SUBS)[:, None]
    group_index = jnp.arange(GROUPS)[None, :]
    quarter = GROUPS // 4
    filler = jnp.zeros((SUBS, GROUPS), jnp.float32)
    lower_sub = filler + (sub_index > 0)
    upper_sub = filler + (sub_index < SUBS - 1)
    lower_group = filler + ((group_index > 0) & (group_index != quarter) & (group_index != 3 * quarter))
    upper_group = filler + ((group_index < GROUPS - 1) & (group_index != quarter - 1) & (group_index != 3 * quarter - 1))
    return (lower_sub, upper_sub, lower_group, upper_group)


def multiplicity(flags):
    pieces = [jnp.broadcast_to(1.0 + face_flag[:, :, None], (SUBS, GROUPS, FACE)) for face_flag in flags]
    pieces.append(jnp.full((SUBS, GROUPS, CONT), 2.0, jnp.float32))
    pieces.append(jnp.ones((SUBS, GROUPS, DIRI), jnp.float32))
    return jnp.concatenate(pieces, axis=2)


def shifted_from_lower(values, axis_number):
    count = values.shape[axis_number]
    zero_slab = jnp.zeros_like(lax.slice_in_dim(values, 0, 1, axis=axis_number))
    return jnp.concatenate([zero_slab, lax.slice_in_dim(values, 0, count - 1, axis=axis_number)], axis=axis_number)


def shifted_from_upper(values, axis_number):
    count = values.shape[axis_number]
    zero_slab = jnp.zeros_like(lax.slice_in_dim(values, 0, 1, axis=axis_number))
    return jnp.concatenate([lax.slice_in_dim(values, 1, count, axis=axis_number), zero_slab], axis=axis_number)


def gather_last(values, order_map):
    return jnp.take_along_axis(values, jnp.broadcast_to(order_map[:, :, None, :], values.shape), axis=3)


def assemble(local_part, orders, inverses, partner, flags):
    lower_face = local_part[..., :FACE]
    upper_face = local_part[..., FACE:2 * FACE]
    group_lower = local_part[..., 2 * FACE:3 * FACE]
    group_upper = local_part[..., 3 * FACE:4 * FACE]
    contact_part = local_part[..., 4 * FACE:4 * FACE + CONT]
    from_lower = shifted_from_lower(gather_last(upper_face, inverses[0]), 0)
    from_upper = gather_last(shifted_from_upper(lower_face, 0), orders[0])
    from_group_lower = shifted_from_lower(gather_last(group_upper, inverses[1]), 1) * flags[2][:, :, None, None]
    from_group_upper = gather_last(shifted_from_upper(group_lower, 1), orders[1]) * flags[3][:, :, None, None]
    partner_part = jnp.roll(contact_part, GROUPS // 2, axis=1)
    from_contact = gather_last(partner_part, partner)
    dirichlet = jnp.zeros(local_part.shape[:3] + (DIRI,), jnp.float32)
    received = jnp.concatenate([from_lower, from_upper, from_group_lower, from_group_upper, from_contact, dirichlet], axis=3)
    return local_part + received


def coarse_fix(field_vec, basis_rows, inverse_rows):
    coarse_coef = jnp.einsum('sgmo,sglo->sgml', basis_rows, field_vec, precision=highest)
    alpha_coef = jnp.dot(inverse_rows, coarse_coef.reshape(NCOARSE, NLOAD), precision=highest)
    alpha_coef = alpha_coef.reshape(SUBS, GROUPS, MODES, NLOAD)
    return jnp.einsum('sgml,sgmo->sglo', alpha_coef, basis_rows, precision=highest)


def apply_schur(schur, field_vec):
    rounded = field_vec.reshape(DOMAINS, NLOAD, ORDER).astype(jnp.bfloat16)

    def apply_block(block_pair):
        return jnp.dot(block_pair[1], block_pair[0], preferred_element_type=jnp.float32)

    return lax.map(apply_block, (schur, rounded)).reshape(SUBS, GROUPS, NLOAD, ORDER)


def inner_sum(left, right, weight):
    return jnp.sum(left * right * weight[:, :, None, :], axis=(0, 1, 3))


def reference(schur, coarse_basis, coarse_inverse, coarse_coeff, dual_load, face_order, contact_partner, active_flags, step_codes):
    basis_rows = coarse_basis.reshape(SUBS, GROUPS, MODES, ORDER)
    orders = (face_order[:, 0, :].reshape(SUBS, GROUPS, FACE), face_order[:, 1, :].reshape(SUBS, GROUPS, FACE))
    inverses = (jnp.argsort(orders[0], axis=-1), jnp.argsort(orders[1], axis=-1))
    partner = contact_partner.reshape(SUBS, GROUPS, CONT)
    flags = face_flags()
    weight = 1.0 / multiplicity(flags)
    flag_rows = active_flags.astype(jnp.float32).reshape(SUBS, GROUPS, NLOAD, CONT)
    active = jnp.concatenate([jnp.zeros((SUBS, GROUPS, NLOAD, 4 * FACE), jnp.float32), flag_rows, jnp.zeros((SUBS, GROUPS, NLOAD, DIRI), jnp.float32)], axis=3)
    free_mask = 1.0 - active
    contact_mask = jnp.concatenate([jnp.zeros((4 * FACE,), jnp.float32), jnp.ones((CONT,), jnp.float32), jnp.zeros((DIRI,), jnp.float32)])

    def assembled(local_part):
        return assemble(local_part, orders, inverses, partner, flags)

    def project(field_vec):
        return field_vec - assembled(coarse_fix(field_vec, basis_rows, coarse_inverse))

    def operator(field_vec):
        return project(assembled(apply_schur(schur, project(field_vec))))

    coef_rows = coarse_coeff.reshape(SUBS, GROUPS, MODES, NLOAD)
    start_point = assembled(jnp.einsum('sgml,sgmo->sglo', coef_rows, basis_rows, precision=highest))
    multipliers = jnp.where(contact_mask > 0, jnp.maximum(start_point, 0.0), start_point)
    load_vec = project(assembled(dual_load.reshape(SUBS, GROUPS, NLOAD, ORDER)))
    gradient = operator(multipliers) - load_vec
    direction = free_mask * gradient
    for step_number in range(ITERS):
        step_code = step_codes[:, step_number]
        code_wide = step_code[None, None, :, None]
        free_grad = free_mask * gradient
        chopped = active * jnp.minimum(gradient, 0.0)
        trial_point = multipliers - step_scale * free_grad
        trial_point = jnp.where(contact_mask > 0, jnp.maximum(trial_point, 0.0), trial_point)
        search = jnp.where(code_wide == 0, direction, jnp.where(code_wide == 2, chopped, trial_point - multipliers))
        image_vec = operator(search)
        slope_sum = inner_sum(gradient, search, weight)
        curve_sum = inner_sum(search, image_vec, weight)
        cross_sum = inner_sum(free_grad, image_vec, weight)
        bend_sum = inner_sum(free_mask * image_vec, image_vec, weight)
        length = jnp.where(step_code == 1, -1.0, slope_sum / curve_sum)
        conj_factor = jnp.where(step_code == 0, (cross_sum - length * bend_sum) / curve_sum, 0.0)
        multipliers = multipliers - length[None, None, :, None] * search
        gradient = gradient - length[None, None, :, None] * image_vec
        direction = free_mask * gradient - conj_factor[None, None, :, None] * direction
    return multipliers.reshape(DOMAINS, NLOAD, ORDER), gradient.reshape(DOMAINS, NLOAD, ORDER)
```

```python
import functools

import jax
import jax.numpy as jnp
from jax import lax
from jax.experimental import pallas as pl
from jax.experimental.pallas import tpu as pltpu
from jax.sharding import PartitionSpec as P

FACE = 512
CONT = 256
ORDER = 2560
MODES = 6
NLOAD = 96
ITERS = 3
CON = 4 * FACE
SEGS = ((0, 512), (512, 512), (1024, 512), (1536, 512), (2048, 256), (2304, 256))

F32 = jnp.float32
BF16 = jnp.bfloat16
step_scale = 0.2
AXES = ("sub", "grp")


def sds(shape, dtype=F32):
    return jax.ShapeDtypeStruct(shape, dtype)


def mm(a, b):
    return jnp.dot(a, b, preferred_element_type=F32)


def split2(x):
    hi = x.astype(BF16)
    return hi, (x - hi.astype(F32)).astype(BF16)


def shuffle(x, onehot):
    hi = x.astype(BF16)
    rest = x - hi.astype(F32)
    mid = rest.astype(BF16)
    low = (rest - mid.astype(F32)).astype(BF16)
    return mm(hi, onehot) + mm(mid, onehot) + mm(low, onehot)


def flip(x):
    rows = x.shape[0]
    if rows % 128:
        x = jnp.concatenate([x, jnp.zeros((128 - rows % 128, x.shape[1]), F32)], axis=0)
    return x.T


def cut(width):
    return [(at, min(width, ORDER - at)) for at in range(0, ORDER, width)]


def spread(rows, t_stack):
    hi = rows.astype(BF16).astype(F32)
    stack = jnp.concatenate([hi, hi, rows - hi, jnp.zeros((112, 128), F32)], axis=0)
    return stack.T[:NLOAD].astype(BF16)


def coarse(vh, vl, g):
    gh, gl = split2(g)
    return mm(vh, gh) + mm(vl, gh) + mm(vh, gl)


def project_rows(x, bh, bl):
    xh, xl = split2(x)
    return mm(xh, bh) + mm(xl, bh) + mm(xh, bl)


def lanesum(x):
    return jnp.sum(x, axis=1, keepdims=True)


def message(coef_t, first, second):
    lane = lax.broadcasted_iota(jnp.int32, coef_t.shape, 1)
    full = jnp.where(lane == 6, first, jnp.where(lane == 7, second, coef_t))
    return flip(full)[:8]


def prepare_kernel(
    basis, vp, coeff, srow, scol, grow, gcol, crow, ccol, flags,
    a_s, at_s, a_g, at_g, a_c, at_c, basis_out, act_out, m0, m1, m2, m3, mc,
):
    for row, col, a, at in ((srow, scol, a_s, at_s), (grow, gcol, a_g, at_g), (crow, ccol, a_c, at_c)):
        n = row.shape[1]
        a[...] = (lax.broadcasted_iota(jnp.int32, (n, n), 1) == col[...]).astype(F32).astype(BF16)
        at[...] = (lax.broadcasted_iota(jnp.int32, (n, n), 0) == row[...]).astype(F32).astype(BF16)
    parts = [
        basis[:, 0:512],
        shuffle(basis[:, 512:1024], a_s[...]),
        basis[:, 1024:1536],
        shuffle(basis[:, 1536:2048], a_g[...]),
        shuffle(basis[:, 2048:2304], a_c[...]),
        basis[:, 2304:2560],
    ]
    for (at, width), part in zip(SEGS, parts):
        basis_out[:, at : at + width] = part
    act_out[...] = mm(flags[...].astype(F32).astype(BF16), a_c[...])
    for ref, part in zip((m0, m1, m2, m3), parts):
        ref[0:8, :] = part
        ref[8:16, :] = vp[:, 0:512]
        ref[16:24, :] = vp[:, 512:1024]
        ref[24:32, :] = jnp.zeros((8, 512), F32)
        ref[24:32, 0:128] = coeff[...]
    mc[0:8, :] = parts[4]
    for k in range(4):
        mc[8 + 8 * k : 16 + 8 * k, :] = vp[:, 256 * k : 256 * k + 256]
    mc[40:48, :] = jnp.zeros((8, 256), F32)
    mc[40:48, 0:128] = coeff[...]


def start_kernel(
    basis, vp, coeff, r0, r1, r2, r3, rc,
    t_stack, vh, vl, bh, bl, point, msg,
):
    zero8 = jnp.zeros((8, ORDER), F32)
    pieces = [basis[...]]
    for ref, at in ((r0, 0), (r1, 512), (r2, 1024), (r3, 1536)):
        left = [zero8[:, :at]] if at else []
        pieces.append(jnp.concatenate(left + [ref[0:8, :], zero8[:, at + 512 :]], axis=1))
    pieces.append(jnp.concatenate([zero8[:, :CON], rc[0:8, :], zero8[:, CON + CONT :]], axis=1))
    t = jnp.concatenate(pieces, axis=0)
    th, tl = split2(t)
    t_stack[0:48, :] = th
    t_stack[48:96, :] = tl
    t_stack[96:144, :] = th
    t_stack[144:256, :] = jnp.zeros((112, ORDER), BF16)
    rows = [vp[...]]
    coefs = [coeff[...]]
    for ref in (r0, r1, r2, r3):
        rows.append(jnp.concatenate([ref[8:16, :], ref[16:24, :]], axis=1))
        coefs.append(ref[24:32, 0:128])
    rows.append(jnp.concatenate([rc[8 + 8 * k : 16 + 8 * k, :] for k in range(4)], axis=1))
    coefs.append(rc[40:48, 0:128])
    hi, low = split2(jnp.concatenate(rows, axis=0))
    vh[...] = hi
    vl[...] = low
    bhi, blow = split2(flip(basis[...]))
    bh[...] = bhi
    bl[...] = blow
    factor = spread(jnp.concatenate(coefs, axis=0), t_stack)
    coef_t = jnp.zeros((NLOAD, 128), F32)
    for at, width in SEGS:
        seg = slice(at, at + width)
        x = mm(factor, t_stack[:, seg])
        if at == CON:
            x = jnp.maximum(x, 0.0)
        point[:, seg] = x
        coef_t += project_rows(x, bh[seg, :], bl[seg, :])
    msg[...] = flip(coef_t)[:8]


def rounded_rows(p, seg, at_s, at_g, at_c):
    p = p.astype(BF16)
    back = {512: at_s, 1536: at_g, 2048: at_c}.get(seg)
    if back is not None:
        p = mm(p, back[...]).astype(BF16)
    return p


def first_search_kernel(
    g, vh, vl, u, t_stack, a_s, at_s, at_g, at_c, schur,
    gh, gl, p, z0, z1,
):
    step = pl.program_id(0)

    @pl.when(step == 0)
    def _():
        column = flip(g[...])[96:112]
        row = lax.broadcasted_iota(jnp.int32, column.shape, 0)
        hi, low = split2(jnp.where(row < MODES, column, 0.0))
        gh[...] = hi
        gl[...] = low
        factor = spread(coarse(vh[...], vl[...], g[...]), t_stack)
        for at, width in SEGS:
            seg = slice(at, at + width)
            p[:, seg] = rounded_rows(u[:, seg] - mm(factor, t_stack[:, seg]), at, at_s, at_g, at_c)
        z0[...] = mm(p[...], schur[...])

    @pl.when(step == 1)
    def _():
        z1[...] = shuffle(mm(p[...], schur[...]), a_s[...])


def search_kernel(
    k, g, vh, vl, gh, gl, codes, scal, prev, u, d, t_stack, a_s, at_s, at_g, at_c, schur,
    q, p, coef_u, coef_q, scal_out, z0, z1,
):
    step = pl.program_id(0)

    @pl.when(step == 0)
    def _():
        got = g[...]
        gah, gal = split2(got)
        alpha = mm(vh[...], gah) + mm(vl[...], gah) + mm(vh[...], gal)
        gamma = (mm(gh[...], gah) + mm(gl[...], gah) + mm(gh[...], gal))[:8]
        sums = jnp.sum(got.reshape(128, 8, 128), axis=0)
        coef = jnp.concatenate([alpha, gamma], axis=0)
        coef_u[...] = coef
        scal_out[0:1, :] = sums[7:8]
        scal_out[1:8, :] = jnp.zeros((7, 128), F32)
        if k > 0:
            bend = sums[6:7]
            length, curve, cross = scal[0:1], scal[1:2], scal[2:3]
            both = (codes[k : k + 1] == 0) & (codes[k - 1 : k] == 0)
            factor2 = jnp.where(both, (cross - length * bend) / curve, 0.0)
            mix = jnp.where(factor2 == 0.0, coef, coef - factor2 * prev[...])
            coef_q[...] = mix
            g2 = flip(jnp.broadcast_to(factor2, (8, 128)))[:NLOAD, 0:1]
        else:
            mix = coef
            coef_q[...] = coef
        factor = spread(mix[:48], t_stack)
        for at, width in SEGS:
            seg = slice(at, at + width)
            x = u[:, seg]
            if k > 0:
                x = x - g2 * d[:, seg]
            q[:, seg] = x
            p[:, seg] = rounded_rows(x - mm(factor, t_stack[:, seg]), at, at_s, at_g, at_c)
        z0[...] = mm(p[...], schur[...])

    @pl.when(step == 1)
    def _():
        z1[...] = shuffle(mm(p[...], schur[...]), a_s[...])


def product_kernel(p, a_g, a_c, schur, z2, z3, zc, zd):
    step = pl.program_id(0)
    z = mm(p[...], schur[...])

    @pl.when(step == 0)
    def _():
        z2[...] = z

    @pl.when(step == 1)
    def _():
        z3[...] = shuffle(z, a_g[...])

    @pl.when(step == 2)
    def _():
        zc[...] = shuffle(z[:, :CONT], a_c[...])
        zd[...] = z[:, CONT:]


def image_kernel(
    z0, z1, z2, z3, zc, zd, r0, r1, r2, r3, rc, q, u, weight, coef_u, coef_q, bh, bl,
    image, msg,
):
    coef_t = jnp.zeros((NLOAD, 128), F32)
    curve = jnp.zeros((NLOAD, 1), F32)
    cross = jnp.zeros((NLOAD, 1), F32)
    pairs = ((z0, r0), (z1, r1), (z2, r2), (z3, r3), (zc, rc), (zd, None))
    for (at, width), (own, got) in zip(SEGS, pairs):
        seg = slice(at, at + width)
        x = own[...] if got is None else own[...] + got[...]
        image[:, seg] = x
        coef_t += project_rows(x, bh[seg, :], bl[seg, :])
        xw = x * weight[:, seg]
        curve += lanesum(q[:, seg] * xw)
        cross += lanesum(u[:, seg] * xw)
    rows = message(coef_t, curve, cross)
    row = lax.broadcasted_iota(jnp.int32, (8, 128), 0)
    modes = jnp.where(row < MODES, rows, 0.0)
    fix_q = jnp.sum(coef_q[48:56] * modes, axis=0, keepdims=True)
    fix_u = jnp.sum(coef_u[48:56] * modes, axis=0, keepdims=True)
    msg[...] = rows - jnp.where(row == 6, fix_q, 0.0) - jnp.where(row == 7, fix_u, 0.0)


def less_load_kernel(z0, z1, z2, z3, zc, zd, load, a_s, a_g, a_c, o0, o1, o2, o3, oc, od):
    pairs = ((z0, o0, None), (z1, o1, a_s), (z2, o2, None), (z3, o3, a_g), (zc, oc, a_c), (zd, od, None))
    for (at, width), (own, out, order) in zip(SEGS, pairs):
        x = load[:, at : at + width]
        out[...] = own[...] - (x if order is None else shuffle(x, order[...]))


def first_image_kernel(
    z0, z1, z2, z3, zc, zd, r0, r1, r2, r3, rc, bh, bl,
    image, msg,
):
    coef_t = jnp.zeros((NLOAD, 128), F32)
    pairs = ((z0, r0), (z1, r1), (z2, r2), (z3, r3), (zc, rc), (zd, None))
    for (at, width), (own, got) in zip(SEGS, pairs):
        seg = slice(at, at + width)
        x = own[...] if got is None else own[...] + got[...]
        image[:, seg] = x
        coef_t += project_rows(x, bh[seg, :], bl[seg, :])
    msg[...] = flip(coef_t)[:8]


def next_part(seg, at, codes, m, g, w, act, weight):
    bent = w * w
    if at == CON:
        free = 1.0 - act
        free_grad = free * g
        bent = free * bent
        chopped = act * jnp.minimum(g, 0.0)
        trial = jnp.maximum(m - step_scale * free_grad, 0.0)
    else:
        free_grad = g
        chopped = 0.0
        trial = m - step_scale * g
    u = jnp.where(codes == 0, free_grad, jnp.where(codes == 2, chopped, trial - m))
    return u, lanesum(g * u * weight), lanesum(bent * weight)


def first_update_kernel(
    g, vh, vl, codes, point, image, act, weight, t_stack, bh, bl,
    gradient, u, msg,
):
    factor = spread(coarse(vh[...], vl[...], g[...]), t_stack)
    code = codes[:, 0:1]
    coef_t = jnp.zeros((NLOAD, 128), F32)
    slope = jnp.zeros((NLOAD, 1), F32)
    for at, width in SEGS:
        seg = slice(at, at + width)
        grad = image[:, seg] - mm(factor, t_stack[:, seg])
        gradient[:, seg] = grad
        x, slope_part, _ = next_part(seg, at, code, point[:, seg], grad, grad, act[...], weight[:, seg])
        u[:, seg] = x
        slope += slope_part
        coef_t += project_rows(x, bh[seg, :], bl[seg, :])
    msg[...] = message(coef_t, jnp.zeros((NLOAD, 1), F32), slope)


def lengths(k, g, codes_rows, scal):
    sums = jnp.sum(g.reshape(128, 8, 128), axis=0)
    curve, cross = sums[6:7], sums[7:8]
    length = jnp.where(codes_rows[k : k + 1] == 1, -1.0, scal[0:1] / curve)
    return length, curve, cross


def update_kernel(
    k, g, vh, vl, codes, codes_rows, scal, point, gradient, q, image, act, weight, t_stack, bh, bl,
    point_out, gradient_out, u, scal_out, msg,
):
    got = g[...]
    length, curve, cross = lengths(k, got, codes_rows, scal)
    scal_out[0:1, :] = length
    scal_out[1:2, :] = curve
    scal_out[2:3, :] = cross
    scal_out[3:8, :] = jnp.zeros((5, 128), F32)
    step = flip(jnp.broadcast_to(length, (8, 128)))[:NLOAD, 0:1]
    factor = spread(coarse(vh[...], vl[...], got), t_stack)
    code = codes[:, k + 1 : k + 2]
    coef_t = jnp.zeros((NLOAD, 128), F32)
    slope = jnp.zeros((NLOAD, 1), F32)
    bend = jnp.zeros((NLOAD, 1), F32)
    for at, width in SEGS:
        seg = slice(at, at + width)
        w = image[:, seg] - mm(factor, t_stack[:, seg])
        m = point[:, seg] - step * q[:, seg]
        grad = gradient[:, seg] - step * w
        point_out[:, seg] = m
        gradient_out[:, seg] = grad
        x, slope_part, bend_part = next_part(seg, at, code, m, grad, w, act[...], weight[:, seg])
        u[:, seg] = x
        slope += slope_part
        bend += bend_part
        coef_t += project_rows(x, bh[seg, :], bl[seg, :])
    msg[...] = message(coef_t, bend, slope)


def last_update_kernel(
    k, g, vh, vl, codes_rows, scal, point, gradient, q, image, t_stack, at_s, at_g, at_c,
    point_out, gradient_out,
):
    got = g[...]
    length, _, _ = lengths(k, got, codes_rows, scal)
    step = flip(jnp.broadcast_to(length, (8, 128)))[:NLOAD, 0:1]
    factor = spread(coarse(vh[...], vl[...], got), t_stack)
    for at, width in SEGS:
        seg = slice(at, at + width)
        w = image[:, seg] - mm(factor, t_stack[:, seg])
        m = point[:, seg] - step * q[:, seg]
        grad = gradient[:, seg] - step * w
        back = {512: at_s, 1536: at_g, 2048: at_c}.get(at)
        if back is not None:
            m = shuffle(m, back[...])
            grad = shuffle(grad, back[...])
        point_out[:, seg] = m
        gradient_out[:, seg] = grad


def call(kernel, outs, *operands, flops=0):
    moved = sum(x.size * x.dtype.itemsize for x in operands) + sum(
        o.size * o.dtype.itemsize for o in outs
    )
    return pl.pallas_call(
        kernel,
        out_shape=outs,
        compiler_params=pltpu.CompilerParams(vmem_limit_bytes=48 * 2**20),
        cost_estimate=pl.CostEstimate(flops=flops, bytes_accessed=moved, transcendentals=0),
    )(*operands)


def whole(shape):
    return pl.BlockSpec(shape, lambda i: (0,) * len(shape))


def call_columns(kernel, outs, first, count, *operands):
    schur = operands[-1]
    moved = sum(x.size * x.dtype.itemsize for x in operands[:-1]) + count * FACE * ORDER * 2
    return pl.pallas_call(
        kernel,
        grid=(count,),
        in_specs=[whole(x.shape) for x in operands[:-1]]
        + [pl.BlockSpec((ORDER, FACE), lambda i: (0, first + i))],
        out_specs=[whole(o.shape) for o in outs],
        out_shape=outs,
        compiler_params=pltpu.CompilerParams(vmem_limit_bytes=48 * 2**20),
        cost_estimate=pl.CostEstimate(
            flops=2 * NLOAD * ORDER * FACE * count, bytes_accessed=moved, transcendentals=0
        ),
    )(*operands)


def shards(
    schur,
    coarse_basis,
    coarse_inverse,
    coarse_coeff,
    dual_load,
    face_order,
    contact_partner,
    active_flags,
    step_codes,
):
    subs, groups = lax.axis_size("sub"), lax.axis_size("grp")
    count = subs * groups
    quarter = groups // 4
    i, j = lax.axis_index("sub"), lax.axis_index("grp")
    sub_up = [(s, s + 1) for s in range(subs - 1)]
    grp_up = [(s, s + 1) for s in range(groups - 1) if s + 1 not in (quarter, 3 * quarter)]
    sub_down = [(b, a) for a, b in sub_up]
    grp_down = [(b, a) for a, b in grp_up]
    across = [(s, (s + groups // 2) % groups) for s in range(groups)]

    def exchange(s0, s1, s2, s3, sc):
        r0 = lax.ppermute(s1, "sub", sub_up)
        r1 = lax.ppermute(s0, "sub", sub_down)
        r2 = lax.ppermute(s3, "grp", grp_up)
        r3 = lax.ppermute(s2, "grp", grp_down)
        rc = lax.ppermute(sc, "grp", across)
        return r0, r1, r2, r3, rc

    def gathered(rows):
        return lax.all_to_all(rows, AXES, 0, 0).reshape(count * 8, 128)

    def everywhere(msg):
        return gathered(jnp.broadcast_to(msg[None], (count, 8, 128)))

    def half(flag):
        return jnp.where(flag, 0.5, 1.0).astype(F32)

    def tall(x):
        return jnp.full((1, x[1]), x[0], F32)

    schur_block = schur[0]
    lower_g = (j > 0) & (j != quarter) & (j != 3 * quarter)
    upper_g = (j < groups - 1) & (j != quarter - 1) & (j != 3 * quarter - 1)
    weight = jnp.concatenate(
        [
            tall((half(i > 0), FACE)),
            tall((half(i < subs - 1), FACE)),
            tall((half(lower_g), FACE)),
            tall((half(upper_g), FACE)),
            tall((0.5, CONT)),
            tall((1.0, ORDER - CON - CONT)),
        ],
        axis=1,
    )
    basis = jnp.pad(coarse_basis[0], ((0, 2), (0, 0)))
    coeff = jnp.pad(coarse_coeff[0], ((0, 2), (0, 128 - NLOAD)))
    blocks = coarse_inverse.reshape(MODES, count, MODES)
    vp = jnp.pad(blocks, ((0, 2), (0, 0), (0, 2))).reshape(8, count * 8)
    columns = jnp.pad(blocks.transpose(1, 0, 2), ((0, 0), (0, 2), (NLOAD, 128 - NLOAD - MODES)))
    codes_rows = jnp.pad(step_codes.T, ((0, 8 - ITERS), (0, 128 - NLOAD)))
    partner = jnp.where(j >= groups // 2, contact_partner[0], jnp.arange(CONT, dtype=jnp.int32))

    orders = []
    for order in (face_order[0, 0], face_order[0, 1], partner):
        orders += [order[None, :], order[:, None]]
    sq = [sds((n, n), BF16) for n in (FACE, FACE, FACE, FACE, CONT, CONT)]
    a_s, at_s, a_g, at_g, a_c, at_c, basis, act, m0, m1, m2, m3, mc = call(
        prepare_kernel,
        sq + [sds((8, ORDER)), sds((NLOAD, CONT))] + [sds((32, FACE))] * 4 + [sds((48, CONT))],
        basis, vp, coeff, *orders, active_flags[0],
    )
    t_stack, vh, vl, bh, bl, point, msg = call(
        start_kernel,
        [
            sds((256, ORDER), BF16),
            sds((48, count * 8), BF16),
            sds((48, count * 8), BF16),
            sds((ORDER, 128), BF16),
            sds((ORDER, 128), BF16),
            sds((NLOAD, ORDER)),
            sds((8, 128)),
        ],
        basis, vp, coeff, *exchange(m0, m1, m2, m3, mc),
    )
    field = sds((NLOAD, ORDER))
    faces = [sds((NLOAD, FACE))] * 2
    rest = [sds((NLOAD, FACE))] * 2 + [sds((NLOAD, CONT))] * 2
    rounded = sds((NLOAD, ORDER), BF16)

    got = gathered(msg[None] + columns)
    gh, gl, p, z0, z1 = call_columns(
        first_search_kernel,
        [sds((16, count * 8), BF16)] * 2 + [rounded] + faces,
        0, 2,
        got, vh, vl, point, t_stack, a_s, at_s, at_g, at_c, schur_block,
    )
    z2, z3, zc, zd = call_columns(product_kernel, rest, 2, 3, p, a_g, a_c, schur_block)
    z0, z1, z2, z3, zc, zd = call(
        less_load_kernel,
        faces + rest,
        z0, z1, z2, z3, zc, zd, dual_load[0], a_s, a_g, a_c,
    )
    image, msg = call(
        first_image_kernel,
        [field, sds((8, 128))],
        z0, z1, z2, z3, zc, zd, *exchange(z0, z1, z2, z3, zc), bh, bl,
    )
    got = everywhere(msg)
    gradient, u, msg = call(
        first_update_kernel,
        [field, field, sds((8, 128))],
        got, vh, vl, step_codes, point, image, act, weight, t_stack, bh, bl,
    )
    q = u
    scal = jnp.zeros((8, 128), F32)
    coef_q = jnp.zeros((56, 128), F32)
    for k in range(ITERS):
        got = everywhere(msg)
        q, p, coef_u, coef_q, scal, z0, z1 = call_columns(
            functools.partial(search_kernel, k),
            [field, rounded, sds((56, 128)), sds((56, 128)), sds((8, 128))] + faces,
            0, 2,
            got, vh, vl, gh, gl, codes_rows, scal, coef_q, u, q, t_stack, a_s, at_s, at_g, at_c,
            schur_block,
        )
        z2, z3, zc, zd = call_columns(product_kernel, rest, 2, 3, p, a_g, a_c, schur_block)
        image, msg = call(
            image_kernel,
            [field, sds((8, 128))],
            z0, z1, z2, z3, zc, zd, *exchange(z0, z1, z2, z3, zc),
            q, u, weight, coef_u, coef_q, bh, bl,
        )
        got = everywhere(msg)
        if k < ITERS - 1:
            point, gradient, u, scal, msg = call(
                functools.partial(update_kernel, k),
                [field, field, field, sds((8, 128)), sds((8, 128))],
                got, vh, vl, step_codes, codes_rows, scal, point, gradient, q, image, act, weight,
                t_stack, bh, bl,
            )
        else:
            point, gradient = call(
                functools.partial(last_update_kernel, k),
                [field, field],
                got, vh, vl, codes_rows, scal, point, gradient, q, image, t_stack, at_s, at_g, at_c,
            )
    return (point[None], gradient[None])


def solution(mesh):
    in_specs = (
        P(AXES, None, None),
        P(AXES, None, None),
        P(AXES, None),
        P(AXES, None, None),
        P(AXES, None, None),
        P(AXES, None, None),
        P(AXES, None),
        P(AXES, None, None),
        P(),
    )
    out_specs = (P(AXES, None, None), P(AXES, None, None))
    return jax.shard_map(shards, mesh=mesh, in_specs=in_specs, out_specs=out_specs, check_vma=False)
```

```python
import functools

import jax
import jax.numpy as jnp
from jax import lax
from jax.experimental import pallas as pl
from jax.experimental.pallas import tpu as pltpu
from jax.sharding import PartitionSpec as P

FACE = 512
CONT = 256
ORDER = 2560
MODES = 6
NLOAD = 96
ITERS = 3
CON = 4 * FACE
SEGS = ((0, 512), (512, 512), (1024, 512), (1536, 512), (2048, 256), (2304, 256))

F32 = jnp.float32
BF16 = jnp.bfloat16
step_scale = 0.2
AXES = ("sub", "grp")


def sds(shape, dtype=F32):
    return jax.ShapeDtypeStruct(shape, dtype)


def mm(a, b):
    return jnp.dot(a, b, preferred_element_type=F32)


def split2(x):
    hi = x.astype(BF16)
    return hi, (x - hi.astype(F32)).astype(BF16)


def turned(x, order):
    return lax.dot_general(x, order, (((1,), (1,)), ((), ())), preferred_element_type=F32)


def parts3(x):
    hi = x.astype(BF16)
    rest = x - hi.astype(F32)
    mid = rest.astype(BF16)
    return hi, mid, (rest - mid.astype(F32)).astype(BF16)


def shuffle(x, order):
    return sum(turned(part, order) for part in parts3(x))


def shuffle_back(x, order):
    return sum(mm(part, order) for part in parts3(x))


def flip(x):
    rows = x.shape[0]
    if rows % 128:
        x = jnp.concatenate([x, jnp.zeros((128 - rows % 128, x.shape[1]), F32)], axis=0)
    return x.T


def cut(width):
    return [(at, min(width, ORDER - at)) for at in range(0, ORDER, width)]


def spread(rows):
    hi = rows.astype(BF16).astype(F32)
    stack = jnp.concatenate([hi, hi, rows - hi, jnp.zeros((112, 128), F32)], axis=0)
    return stack.T[:NLOAD].astype(BF16)


def coarse(vh, vl, g):
    gh, gl = split2(g)
    return mm(vh, gh) + mm(vl, gh) + mm(vh, gl)


def project_rows(x, bh, bl):
    xh, xl = split2(x)
    return mm(xh, bh) + mm(xl, bh) + mm(xh, bl)


def lanesum(x):
    return jnp.sum(x, axis=1, keepdims=True)


def message(coef_t, first, second):
    lane = lax.broadcasted_iota(jnp.int32, coef_t.shape, 1)
    full = jnp.where(lane == 6, first, jnp.where(lane == 7, second, coef_t))
    return flip(full)[:8]


def send_faces(par, faces, refs):
    even_i, even_j = par[0:1, :] > 0.5, par[1:2, :] > 0.5
    f0, f1, f2, f3 = faces
    refs[0][...] = jnp.where(even_i, f1, f0)
    refs[1][...] = jnp.where(even_i, f0, f1)
    refs[2][...] = jnp.where(even_j, f3, f2)
    refs[3][...] = jnp.where(even_j, f2, f3)


def take_faces(par, refs):
    even_i, even_j = par[0:1, :] > 0.5, par[1:2, :] > 0.5
    xa, xb, ya, yb = (ref[...] for ref in refs)
    return (
        jnp.where(even_i, xb, xa),
        jnp.where(even_i, xa, xb),
        jnp.where(even_j, yb, ya),
        jnp.where(even_j, ya, yb),
    )


def weight(par, at):
    if at < CON:
        row = 2 + at // FACE
        return par[row : row + 1, :]
    return 0.5 if at == CON else 1.0


def padded(x, rows, columns):
    if x.shape[1] < columns:
        x = jnp.concatenate([x, jnp.zeros((x.shape[0], columns - x.shape[1]), F32)], axis=1)
    if x.shape[0] < rows:
        x = jnp.concatenate([x, jnp.zeros((rows - x.shape[0], columns), F32)], axis=0)
    return x


def prepare_kernel(
    basis, vp, coeff, face_rows, contact_row, flags, codes, par,
    o_s, o_g, o_c, basis_out, coeff_out, act_out, code_columns, code_rows, xa, xb, ya, yb, mc,
):
    for row, out in ((face_rows[0:1, :], o_s), (face_rows[1:2, :], o_g), (contact_row[...], o_c)):
        n = row.shape[1]
        out[...] = (lax.broadcasted_iota(jnp.int32, (n, n), 0) == row).astype(F32).astype(BF16)
    rows = padded(basis[...], 8, ORDER)
    parts = [
        rows[:, 0:512],
        shuffle(rows[:, 512:1024], o_s[...]),
        rows[:, 1024:1536],
        shuffle(rows[:, 1536:2048], o_g[...]),
        shuffle(rows[:, 2048:2304], o_c[...]),
        rows[:, 2304:2560],
    ]
    for (at, width), part in zip(SEGS, parts):
        basis_out[:, at : at + width] = part
    act_out[...] = turned(flags[...].astype(F32).astype(BF16), o_c[...])
    code = padded(codes[...].astype(F32), NLOAD, 128)
    code_columns[...] = code
    code_rows[...] = flip(code)[:8]
    inv = vp[...]
    own = padded(coeff[...], 8, 512)
    coeff_out[...] = own[:, :128]
    extra = [inv[:, 0:512], inv[:, 512:1024], own]
    send_faces(
        par,
        [jnp.concatenate([part] + extra, axis=0) for part in parts[:4]],
        (xa, xb, ya, yb),
    )
    mc[0:8, :] = parts[4]
    for k in range(4):
        mc[8 + 8 * k : 16 + 8 * k, :] = inv[:, 256 * k : 256 * k + 256]
    mc[40:48, :] = own[:, :256]


def start_kernel(
    basis, vp, coeff, par, columns, xa, xb, ya, yb, rc,
    t_stack, vh, vl, bh, bl, point, msg,
):
    zero8 = jnp.zeros((8, ORDER), F32)
    pieces = [basis[...]]
    rows = [vp[...]]
    coefs = [coeff[...]]
    for k, got in enumerate(take_faces(par, (xa, xb, ya, yb))):
        at = FACE * k
        left = [zero8[:, :at]] if at else []
        pieces.append(jnp.concatenate(left + [got[0:8, :], zero8[:, at + FACE :]], axis=1))
        rows.append(jnp.concatenate([got[8:16, :], got[16:24, :]], axis=1))
        coefs.append(got[24:32, 0:128])
    pieces.append(jnp.concatenate([zero8[:, :CON], rc[0:8, :], zero8[:, CON + CONT :]], axis=1))
    rows.append(jnp.concatenate([rc[8 + 8 * k : 16 + 8 * k, :] for k in range(4)], axis=1))
    coefs.append(rc[40:48, 0:128])
    th, tl = split2(jnp.concatenate(pieces, axis=0))
    t_stack[0:48, :] = th
    t_stack[48:96, :] = tl
    t_stack[96:144, :] = th
    t_stack[144:256, :] = jnp.zeros((112, ORDER), BF16)
    hi, low = split2(jnp.concatenate(rows, axis=0))
    vh[...] = hi
    vl[...] = low
    bhi, blow = split2(flip(basis[...]))
    bh[...] = bhi
    bl[...] = blow
    factor = spread(jnp.concatenate(coefs, axis=0))
    coef_t = jnp.zeros((NLOAD, 128), F32)
    for at, width in SEGS:
        seg = slice(at, at + width)
        x = mm(factor, t_stack[:, seg])
        if at == CON:
            x = jnp.maximum(x, 0.0)
        point[:, seg] = x
        coef_t += project_rows(x, bh[seg, :], bl[seg, :])
    msg[...] = columns[...] + flip(coef_t)[:8][None]


def rounded(x, at, orders):
    x = x.astype(BF16)
    order = dict(zip((512, 1536, 2048), orders)).get(at)
    return x if order is None else mm(x, order[...]).astype(BF16)


def product_block(p, schur, orders, z, load=None):
    step = pl.program_id(0)
    y = mm(p[...], schur[...])
    if load is not None:
        y = y - load[...]
    for n in range(5):

        @pl.when(step == n)
        def _():
            x = y
            if n == 4:
                x = jnp.concatenate([shuffle(x[:, :CONT], orders[2][...]), x[:, CONT:]], axis=1)
            elif n in (1, 3):
                x = shuffle(x, orders[n // 2][...])
            z[:, FACE * n : FACE * (n + 1)] = x


def send_product(par, z, xa, xb, ya, yb, xc):
    @pl.when(pl.program_id(0) == 4)
    def _():
        send_faces(par, [z[:, FACE * n : FACE * (n + 1)] for n in range(4)], (xa, xb, ya, yb))
        xc[...] = z[:, CON : CON + CONT]


def first_search_kernel(
    g, vh, vl, par, u, t_stack, o_s, o_g, o_c, load, schur,
    gh, gl, z, xa, xb, ya, yb, xc, p,
):
    orders = (o_s, o_g, o_c)

    @pl.when(pl.program_id(0) == 0)
    def _():
        column = flip(g[...])[96:112]
        row = lax.broadcasted_iota(jnp.int32, column.shape, 0)
        hi, low = split2(jnp.where(row < MODES, column, 0.0))
        gh[...] = hi
        gl[...] = low
        factor = spread(coarse(vh[...], vl[...], g[...]))
        for at, width in SEGS:
            seg = slice(at, at + width)
            p[:, seg] = rounded(u[:, seg] - mm(factor, t_stack[:, seg]), at, orders)

    product_block(p, schur, orders, z, load)
    send_product(par, z, xa, xb, ya, yb, xc)


def search_kernel(
    k, g, vh, vl, gh, gl, codes, scal, prev, par, u, d, t_stack, o_s, o_g, o_c, schur,
    coef_u, coef_q, scal_out, q, z, xa, xb, ya, yb, xc, p,
):
    orders = (o_s, o_g, o_c)

    @pl.when(pl.program_id(0) == 0)
    def _():
        got = g[...]
        gah, gal = split2(got)
        alpha = mm(vh[...], gah) + mm(vl[...], gah) + mm(vh[...], gal)
        gamma = (mm(gh[...], gah) + mm(gl[...], gah) + mm(gh[...], gal))[:8]
        sums = jnp.sum(got.reshape(128, 8, 128), axis=0)
        mix = jnp.concatenate([alpha, gamma], axis=0)
        coef_u[...] = mix
        scal_out[0:1, :] = sums[7:8]
        scal_out[1:8, :] = jnp.zeros((7, 128), F32)
        if k > 0:
            bend = sums[6:7]
            length, curve, cross = scal[0:1], scal[1:2], scal[2:3]
            both = (codes[k : k + 1] == 0) & (codes[k - 1 : k] == 0)
            factor2 = jnp.where(both, (cross - length * bend) / curve, 0.0)
            mix = jnp.where(factor2 == 0.0, mix, mix - factor2 * prev[...])
            g2 = flip(jnp.broadcast_to(factor2, (8, 128)))[:NLOAD, 0:1]
        coef_q[...] = mix
        factor = spread(mix[:48])
        for at, width in SEGS:
            seg = slice(at, at + width)
            x = u[:, seg]
            if k > 0:
                x = x - g2 * d[:, seg]
            q[:, seg] = x
            p[:, seg] = rounded(x - mm(factor, t_stack[:, seg]), at, orders)

    product_block(p, schur, orders, z)
    send_product(par, z, xa, xb, ya, yb, xc)


def image_kernel(
    z, xa, xb, ya, yb, rc, par, q, u, coef_u, coef_q, bh, bl,
    image, msg,
):
    coef_t = jnp.zeros((NLOAD, 128), F32)
    curve = jnp.zeros((NLOAD, 1), F32)
    cross = jnp.zeros((NLOAD, 1), F32)
    coming = take_faces(par, (xa, xb, ya, yb)) + (rc[...], None)
    for (at, width), got in zip(SEGS, coming):
        seg = slice(at, at + width)
        x = z[:, seg] if got is None else z[:, seg] + got
        image[:, seg] = x
        coef_t += project_rows(x, bh[seg, :], bl[seg, :])
        xw = x * weight(par, at)
        curve += lanesum(q[:, seg] * xw)
        cross += lanesum(u[:, seg] * xw)
    rows = message(coef_t, curve, cross)
    row = lax.broadcasted_iota(jnp.int32, (8, 128), 0)
    modes = jnp.where(row < MODES, rows, 0.0)
    fix_q = jnp.sum(coef_q[48:56] * modes, axis=0, keepdims=True)
    fix_u = jnp.sum(coef_u[48:56] * modes, axis=0, keepdims=True)
    rows = rows - jnp.where(row == 6, fix_q, 0.0) - jnp.where(row == 7, fix_u, 0.0)
    msg[...] = jnp.broadcast_to(rows[None], msg.shape)


def first_image_kernel(z, xa, xb, ya, yb, rc, par, bh, bl, image, msg):
    coef_t = jnp.zeros((NLOAD, 128), F32)
    coming = take_faces(par, (xa, xb, ya, yb)) + (rc[...], None)
    for (at, width), got in zip(SEGS, coming):
        seg = slice(at, at + width)
        x = z[:, seg] if got is None else z[:, seg] + got
        image[:, seg] = x
        coef_t += project_rows(x, bh[seg, :], bl[seg, :])
    msg[...] = jnp.broadcast_to(flip(coef_t)[:8][None], msg.shape)


def next_part(seg, at, codes, m, g, w, act, weight):
    bent = w * w
    if at == CON:
        free = 1.0 - act
        free_grad = free * g
        bent = free * bent
        chopped = act * jnp.minimum(g, 0.0)
        trial = jnp.maximum(m - step_scale * free_grad, 0.0)
    else:
        free_grad = g
        chopped = 0.0
        trial = m - step_scale * g
    u = jnp.where(codes == 0, free_grad, jnp.where(codes == 2, chopped, trial - m))
    return u, lanesum(g * u * weight), lanesum(bent * weight)


def first_update_kernel(
    g, vh, vl, codes, point, image, act, par, t_stack, bh, bl,
    gradient, u, msg,
):
    factor = spread(coarse(vh[...], vl[...], g[...]))
    code = codes[:, 0:1]
    coef_t = jnp.zeros((NLOAD, 128), F32)
    slope = jnp.zeros((NLOAD, 1), F32)
    for at, width in SEGS:
        seg = slice(at, at + width)
        grad = image[:, seg] - mm(factor, t_stack[:, seg])
        gradient[:, seg] = grad
        x, slope_part, _ = next_part(seg, at, code, point[:, seg], grad, grad, act[...], weight(par, at))
        u[:, seg] = x
        slope += slope_part
        coef_t += project_rows(x, bh[seg, :], bl[seg, :])
    rows = message(coef_t, jnp.zeros((NLOAD, 1), F32), slope)
    msg[...] = jnp.broadcast_to(rows[None], msg.shape)


def lengths(k, g, codes_rows, scal):
    sums = jnp.sum(g.reshape(128, 8, 128), axis=0)
    curve, cross = sums[6:7], sums[7:8]
    length = jnp.where(codes_rows[k : k + 1] == 1, -1.0, scal[0:1] / curve)
    return length, curve, cross


def update_kernel(
    k, g, vh, vl, codes, codes_rows, scal, point, gradient, q, image, act, par, t_stack, bh, bl,
    point_out, gradient_out, u, scal_out, msg,
):
    got = g[...]
    length, curve, cross = lengths(k, got, codes_rows, scal)
    scal_out[0:1, :] = length
    scal_out[1:2, :] = curve
    scal_out[2:3, :] = cross
    scal_out[3:8, :] = jnp.zeros((5, 128), F32)
    step = flip(jnp.broadcast_to(length, (8, 128)))[:NLOAD, 0:1]
    factor = spread(coarse(vh[...], vl[...], got))
    code = codes[:, k + 1 : k + 2]
    coef_t = jnp.zeros((NLOAD, 128), F32)
    slope = jnp.zeros((NLOAD, 1), F32)
    bend = jnp.zeros((NLOAD, 1), F32)
    for at, width in SEGS:
        seg = slice(at, at + width)
        w = image[:, seg] - mm(factor, t_stack[:, seg])
        m = point[:, seg] - step * q[:, seg]
        grad = gradient[:, seg] - step * w
        point_out[:, seg] = m
        gradient_out[:, seg] = grad
        x, slope_part, bend_part = next_part(seg, at, code, m, grad, w, act[...], weight(par, at))
        u[:, seg] = x
        slope += slope_part
        bend += bend_part
        coef_t += project_rows(x, bh[seg, :], bl[seg, :])
    msg[...] = jnp.broadcast_to(message(coef_t, bend, slope)[None], msg.shape)


def last_update_kernel(
    k, g, vh, vl, codes_rows, scal, point, gradient, q, image, t_stack, o_s, o_g, o_c,
    point_out, gradient_out,
):
    got = g[...]
    length, _, _ = lengths(k, got, codes_rows, scal)
    step = flip(jnp.broadcast_to(length, (8, 128)))[:NLOAD, 0:1]
    factor = spread(coarse(vh[...], vl[...], got))
    for at, width in SEGS:
        seg = slice(at, at + width)
        w = image[:, seg] - mm(factor, t_stack[:, seg])
        m = point[:, seg] - step * q[:, seg]
        grad = gradient[:, seg] - step * w
        order = {512: o_s, 1536: o_g, 2048: o_c}.get(at)
        if order is not None:
            m = shuffle_back(m, order[...])
            grad = shuffle_back(grad, order[...])
        point_out[:, seg] = m
        gradient_out[:, seg] = grad


VMEM_BYTES = 24 * 2**20


def call(kernel, outs, *operands, flops=0):
    moved = sum(x.size * x.dtype.itemsize for x in operands) + sum(
        o.size * o.dtype.itemsize for o in outs
    )
    return pl.pallas_call(
        kernel,
        out_shape=outs,
        compiler_params=pltpu.CompilerParams(vmem_limit_bytes=VMEM_BYTES),
        cost_estimate=pl.CostEstimate(flops=flops, bytes_accessed=moved, transcendentals=0),
    )(*operands)


def whole(shape):
    return pl.BlockSpec(shape, lambda i: (0,) * len(shape))


def columns_of(rows):
    return pl.BlockSpec((rows, FACE), lambda i: (0, i))


def call_columns(kernel, outs, fixed, streamed):
    return pl.pallas_call(
        kernel,
        grid=(ORDER // FACE,),
        in_specs=[whole(x.shape) for x in fixed] + [columns_of(x.shape[0]) for x in streamed],
        out_specs=[whole(o.shape) for o in outs],
        out_shape=outs,
        scratch_shapes=[pltpu.VMEM((NLOAD, ORDER), BF16)],
        compiler_params=pltpu.CompilerParams(vmem_limit_bytes=VMEM_BYTES),
        cost_estimate=pl.CostEstimate(
            flops=2 * NLOAD * ORDER * ORDER, bytes_accessed=30 * 2**20, transcendentals=0
        ),
    )(*fixed, *streamed)


def shards(
    schur,
    coarse_basis,
    coarse_inverse,
    coarse_coeff,
    dual_load,
    face_order,
    contact_partner,
    active_flags,
    step_codes,
):
    subs, groups = lax.axis_size("sub"), lax.axis_size("grp")
    count = subs * groups
    quarter = groups // 4
    i, j = lax.axis_index("sub"), lax.axis_index("grp")
    sub_pairs = [(s, s + 1) for s in range(subs - 1)]
    grp_pairs = [(s, s + 1) for s in range(groups - 1) if s + 1 not in (quarter, 3 * quarter)]
    across = [(s, (s + groups // 2) % groups) for s in range(groups)]

    def swaps(pairs, odd):
        chosen = [(a, b) for a, b in pairs if a % 2 == odd]
        return chosen + [(b, a) for a, b in chosen]

    def exchange(xa, xb, ya, yb, xc):
        rc = lax.ppermute(xc, "grp", across)
        ra = lax.ppermute(xa, "sub", swaps(sub_pairs, 0))
        rb = lax.ppermute(xb, "sub", swaps(sub_pairs, 1))
        sb = lax.ppermute(yb, "grp", swaps(grp_pairs, 1))
        sa = lax.ppermute(ya, "grp", swaps(grp_pairs, 0))
        return ra, rb, sa, sb, rc

    def gathered(rows):
        return lax.all_to_all(rows, AXES, 0, 0).reshape(count * 8, 128)

    def half(flag):
        return jnp.where(flag, 0.5, 1.0).astype(F32)

    def wide(value, width=FACE):
        return jnp.full((1, width), value, F32)

    schur_block = schur[0]
    lower_g = (j > 0) & (j != quarter) & (j != 3 * quarter)
    upper_g = (j < groups - 1) & (j != quarter - 1) & (j != 3 * quarter - 1)
    par = jnp.concatenate(
        [
            wide((i % 2 == 0).astype(F32)),
            wide((j % 2 == 0).astype(F32)),
            wide(half(i > 0)),
            wide(half(i < subs - 1)),
            wide(half(lower_g)),
            wide(half(upper_g)),
            jnp.zeros((2, FACE), F32),
        ]
    )
    blocks = coarse_inverse.reshape(MODES, count, MODES)
    vp = jnp.pad(blocks, ((0, 2), (0, 0), (0, 2))).reshape(8, count * 8)
    columns = jnp.pad(blocks.transpose(1, 0, 2), ((0, 0), (0, 2), (NLOAD, 128 - NLOAD - MODES)))
    partner = jnp.where(j >= groups // 2, contact_partner, jnp.arange(CONT, dtype=jnp.int32)[None])

    field = sds((NLOAD, ORDER))
    small = sds((8, 128))
    ready = sds((count, 8, 128))
    buffers = [sds((NLOAD, FACE))] * 4 + [sds((NLOAD, CONT))]

    o_s, o_g, o_c, basis, coeff, act, code_columns, code_rows, *faces = call(
        prepare_kernel,
        [sds((FACE, FACE), BF16)] * 2
        + [sds((CONT, CONT), BF16), sds((8, ORDER)), small, sds((NLOAD, CONT))]
        + [sds((NLOAD, 128)), small]
        + [sds((32, FACE))] * 4
        + [sds((48, CONT))],
        coarse_basis[0], vp, coarse_coeff[0], face_order[0], partner, active_flags[0], step_codes, par,
    )
    t_stack, vh, vl, bh, bl, point, msg = call(
        start_kernel,
        [sds((256, ORDER), BF16)]
        + [sds((48, count * 8), BF16)] * 2
        + [sds((ORDER, 128), BF16)] * 2
        + [field, ready],
        basis, vp, coeff, par, columns, *exchange(*faces),
    )
    orders = (o_s, o_g, o_c)

    got = gathered(msg)
    gh, gl, z, *faces = call_columns(
        first_search_kernel,
        [sds((16, count * 8), BF16)] * 2 + [field] + buffers,
        (got, vh, vl, par, point, t_stack) + orders,
        (dual_load[0], schur_block),
    )
    image, msg = call(first_image_kernel, [field, ready], z, *exchange(*faces), par, bh, bl)
    got = gathered(msg)
    gradient, u, msg = call(
        first_update_kernel,
        [field, field, ready],
        got, vh, vl, code_columns, point, image, act, par, t_stack, bh, bl,
    )
    q = u
    scal = jnp.zeros((8, 128), F32)
    coef_q = jnp.zeros((56, 128), F32)
    for k in range(ITERS):
        got = gathered(msg)
        coef_u, coef_q, scal, q, z, *faces = call_columns(
            functools.partial(search_kernel, k),
            [sds((56, 128))] * 2 + [small, field, field] + buffers,
            (got, vh, vl, gh, gl, code_rows, scal, coef_q, par, u, q, t_stack) + orders,
            (schur_block,),
        )
        image, msg = call(
            image_kernel,
            [field, ready],
            z, *exchange(*faces), par, q, u, coef_u, coef_q, bh, bl,
        )
        got = gathered(msg)
        if k < ITERS - 1:
            point, gradient, u, scal, msg = call(
                functools.partial(update_kernel, k),
                [field, field, field, small, ready],
                got, vh, vl, code_columns, code_rows, scal, point, gradient, q, image, act, par,
                t_stack, bh, bl,
            )
        else:
            point, gradient = call(
                functools.partial(last_update_kernel, k),
                [field, field],
                got, vh, vl, code_rows, scal, point, gradient, q, image, t_stack, *orders,
            )
    return (point[None], gradient[None])


def solution(mesh):
    in_specs = (
        P(AXES, None, None),
        P(AXES, None, None),
        P(AXES, None),
        P(AXES, None, None),
        P(AXES, None, None),
        P(AXES, None, None),
        P(AXES, None),
        P(AXES, None, None),
        P(),
    )
    out_specs = (P(AXES, None, None), P(AXES, None, None))
    return jax.shard_map(shards, mesh=mesh, in_specs=in_specs, out_specs=out_specs, check_vma=False)
```

```python
import functools

import jax
import jax.numpy as jnp
from jax import lax
from jax.experimental import pallas as pl
from jax.experimental.pallas import tpu as pltpu
from jax.sharding import PartitionSpec as P

FACE = 512
CONT = 256
ORDER = 2560
MODES = 6
NLOAD = 96
ITERS = 3
CON = 4 * FACE
SEGS = ((0, 512), (512, 512), (1024, 512), (1536, 512), (2048, 256), (2304, 256))

F32 = jnp.float32
BF16 = jnp.bfloat16
step_scale = 0.2
AXES = ("sub", "grp")


def sds(shape, dtype=F32):
    return jax.ShapeDtypeStruct(shape, dtype)


def mm(a, b):
    return jnp.dot(a, b, preferred_element_type=F32)


def split2(x):
    hi = x.astype(BF16)
    return hi, (x - hi.astype(F32)).astype(BF16)


def turned(x, order):
    return lax.dot_general(x, order, (((1,), (1,)), ((), ())), preferred_element_type=F32)


def parts3(x):
    hi = x.astype(BF16)
    rest = x - hi.astype(F32)
    mid = rest.astype(BF16)
    return hi, mid, (rest - mid.astype(F32)).astype(BF16)


def shuffle(x, order):
    return sum(turned(part, order) for part in parts3(x))


def shuffle_back(x, order):
    return sum(mm(part, order) for part in parts3(x))


def flip(x):
    rows = x.shape[0]
    if rows % 128:
        x = jnp.concatenate([x, jnp.zeros((128 - rows % 128, x.shape[1]), F32)], axis=0)
    return x.T


def cut(width):
    return [(at, min(width, ORDER - at)) for at in range(0, ORDER, width)]


def spread(rows):
    hi = rows.astype(BF16).astype(F32)
    stack = jnp.concatenate([hi, hi, rows - hi, jnp.zeros((112, 128), F32)], axis=0)
    return stack.T[:NLOAD].astype(BF16)


def coarse(vh, vl, g):
    gh, gl = split2(g)
    return mm(vh, gh) + mm(vl, gh) + mm(vh, gl)


def project_rows(x, bh, bl):
    xh, xl = split2(x)
    return mm(xh, bh) + mm(xl, bh) + mm(xh, bl)


def lanesum(x):
    return jnp.sum(x, axis=1, keepdims=True)


def message(coef_t, first, second):
    lane = lax.broadcasted_iota(jnp.int32, coef_t.shape, 1)
    full = jnp.where(lane == 6, first, jnp.where(lane == 7, second, coef_t))
    return flip(full)[:8]


def send_faces(par, faces, refs):
    even_i, even_j = par[0:1, :] > 0.5, par[1:2, :] > 0.5
    f0, f1, f2, f3 = faces
    refs[0][...] = jnp.where(even_i, f1, f0)
    refs[1][...] = jnp.where(even_i, f0, f1)
    refs[2][...] = jnp.where(even_j, f3, f2)
    refs[3][...] = jnp.where(even_j, f2, f3)


def take_faces(par, refs):
    even_i, even_j = par[0:1, :] > 0.5, par[1:2, :] > 0.5
    xa, xb, ya, yb = (ref[...] for ref in refs)
    return (
        jnp.where(even_i, xb, xa),
        jnp.where(even_i, xa, xb),
        jnp.where(even_j, yb, ya),
        jnp.where(even_j, ya, yb),
    )


def weight(par, at):
    if at < CON:
        row = 2 + at // FACE
        return par[row : row + 1, :]
    return 0.5 if at == CON else 1.0


def padded(x, rows, columns):
    if x.shape[1] < columns:
        x = jnp.concatenate([x, jnp.zeros((x.shape[0], columns - x.shape[1]), F32)], axis=1)
    if x.shape[0] < rows:
        x = jnp.concatenate([x, jnp.zeros((rows - x.shape[0], columns), F32)], axis=0)
    return x


def prepare_kernel(
    basis, vp, coeff, face_rows, contact_row, flags, codes, par,
    o_s, o_g, o_c, basis_out, coeff_out, act_out, code_columns, code_rows, mc, xb, xa, yb, ya,
):
    for row, out in ((face_rows[0:1, :], o_s), (face_rows[1:2, :], o_g), (contact_row[...], o_c)):
        n = row.shape[1]
        out[...] = (lax.broadcasted_iota(jnp.int32, (n, n), 0) == row).astype(F32).astype(BF16)
    rows = padded(basis[...], 8, ORDER)
    parts = [
        rows[:, 0:512],
        shuffle(rows[:, 512:1024], o_s[...]),
        rows[:, 1024:1536],
        shuffle(rows[:, 1536:2048], o_g[...]),
        shuffle(rows[:, 2048:2304], o_c[...]),
        rows[:, 2304:2560],
    ]
    for (at, width), part in zip(SEGS, parts):
        basis_out[:, at : at + width] = part
    act_out[...] = turned(flags[...].astype(F32).astype(BF16), o_c[...])
    code = padded(codes[...].astype(F32), NLOAD, 128)
    code_columns[...] = code
    code_rows[...] = flip(code)[:8]
    inv = vp[...]
    own = padded(coeff[...], 8, 512)
    coeff_out[...] = own[:, :128]
    extra = [inv[:, 0:512], inv[:, 512:1024], own]
    send_faces(
        par,
        [jnp.concatenate([part] + extra, axis=0) for part in parts[:4]],
        (xa, xb, ya, yb),
    )
    mc[0:8, :] = parts[4]
    for k in range(4):
        mc[8 + 8 * k : 16 + 8 * k, :] = inv[:, 256 * k : 256 * k + 256]
    mc[40:48, :] = own[:, :256]


def start_kernel(
    basis, vp, coeff, par, columns, early_schur, early_load, xa, xb, ya, yb, rc,
    t_stack, vh, vl, bh, bl, point, msg,
):
    del early_schur, early_load
    zero8 = jnp.zeros((8, ORDER), F32)
    pieces = [basis[...]]
    rows = [vp[...]]
    coefs = [coeff[...]]
    for k, got in enumerate(take_faces(par, (xa, xb, ya, yb))):
        at = FACE * k
        left = [zero8[:, :at]] if at else []
        pieces.append(jnp.concatenate(left + [got[0:8, :], zero8[:, at + FACE :]], axis=1))
        rows.append(jnp.concatenate([got[8:16, :], got[16:24, :]], axis=1))
        coefs.append(got[24:32, 0:128])
    pieces.append(jnp.concatenate([zero8[:, :CON], rc[0:8, :], zero8[:, CON + CONT :]], axis=1))
    rows.append(jnp.concatenate([rc[8 + 8 * k : 16 + 8 * k, :] for k in range(4)], axis=1))
    coefs.append(rc[40:48, 0:128])
    th, tl = split2(jnp.concatenate(pieces, axis=0))
    t_stack[0:48, :] = th
    t_stack[48:96, :] = tl
    t_stack[96:144, :] = th
    t_stack[144:256, :] = jnp.zeros((112, ORDER), BF16)
    hi, low = split2(jnp.concatenate(rows, axis=0))
    vh[...] = hi
    vl[...] = low
    bhi, blow = split2(flip(basis[...]))
    bh[...] = bhi
    bl[...] = blow
    factor = spread(jnp.concatenate(coefs, axis=0))
    coef_t = jnp.zeros((NLOAD, 128), F32)
    for at, width in SEGS:
        seg = slice(at, at + width)
        x = mm(factor, t_stack[:, seg])
        if at == CON:
            x = jnp.maximum(x, 0.0)
        point[:, seg] = x
        coef_t += project_rows(x, bh[seg, :], bl[seg, :])
    msg[...] = columns[...] + flip(coef_t)[:8][None]


def rounded(x, at, orders):
    x = x.astype(BF16)
    order = dict(zip((512, 1536, 2048), orders)).get(at)
    return x if order is None else mm(x, order[...]).astype(BF16)


def product(p, schur, orders, par, z, xc, xb, xa, yb, ya, load=None):
    faces = {}
    for n in (4, 0, 1, 2, 3):
        seg = slice(FACE * n, FACE * (n + 1))
        x = mm(p[...], schur[:, seg])
        if load is not None:
            x = x - load[:, seg]
        if n == 4:
            x = jnp.concatenate([shuffle(x[:, :CONT], orders[2][...]), x[:, CONT:]], axis=1)
        elif n in (1, 3):
            x = shuffle(x, orders[n // 2][...])
        z[:, seg] = x
    send_faces(par, [z[:, FACE * n : FACE * (n + 1)] for n in range(4)], (xa, xb, ya, yb))
    xc[...] = z[:, CON : CON + CONT]


def first_search_kernel(
    g, vh, vl, par, u, t_stack, o_s, o_g, o_c, load, schur,
    gh, gl, z, xc, xb, xa, yb, ya, p,
):
    orders = (o_s, o_g, o_c)

    column = flip(g[...])[96:112]
    row = lax.broadcasted_iota(jnp.int32, column.shape, 0)
    hi, low = split2(jnp.where(row < MODES, column, 0.0))
    gh[...] = hi
    gl[...] = low
    factor = spread(coarse(vh[...], vl[...], g[...]))
    for at, width in SEGS:
        seg = slice(at, at + width)
        p[:, seg] = rounded(u[:, seg] - mm(factor, t_stack[:, seg]), at, orders)
    product(p, schur, orders, par, z, xc, xb, xa, yb, ya, load)


def search_kernel(
    k, g, vh, vl, gh, gl, codes, scal, prev, par, u, d, t_stack, o_s, o_g, o_c, schur,
    coef_u, coef_q, scal_out, q, z, xc, xb, xa, yb, ya, p,
):
    orders = (o_s, o_g, o_c)

    got = g[...]
    gah, gal = split2(got)
    alpha = mm(vh[...], gah) + mm(vl[...], gah) + mm(vh[...], gal)
    gamma = (mm(gh[...], gah) + mm(gl[...], gah) + mm(gh[...], gal))[:8]
    sums = jnp.sum(got.reshape(128, 8, 128), axis=0)
    mix = jnp.concatenate([alpha, gamma], axis=0)
    coef_u[...] = mix
    scal_out[0:1, :] = sums[7:8]
    scal_out[1:8, :] = jnp.zeros((7, 128), F32)
    if k > 0:
        bend = sums[6:7]
        length, curve, cross = scal[0:1], scal[1:2], scal[2:3]
        both = (codes[k : k + 1] == 0) & (codes[k - 1 : k] == 0)
        factor2 = jnp.where(both, (cross - length * bend) / curve, 0.0)
        mix = jnp.where(factor2 == 0.0, mix, mix - factor2 * prev[...])
        g2 = flip(jnp.broadcast_to(factor2, (8, 128)))[:NLOAD, 0:1]
    coef_q[...] = mix
    factor = spread(mix[:48])
    for at, width in SEGS:
        seg = slice(at, at + width)
        x = u[:, seg]
        if k > 0:
            x = x - g2 * d[:, seg]
        q[:, seg] = x
        p[:, seg] = rounded(x - mm(factor, t_stack[:, seg]), at, orders)

    product(p, schur, orders, par, z, xc, xb, xa, yb, ya)


def image_kernel(
    z, xa, xb, ya, yb, rc, par, q, u, coef_u, coef_q, bh, bl,
    image, msg,
):
    coef_t = jnp.zeros((NLOAD, 128), F32)
    curve = jnp.zeros((NLOAD, 1), F32)
    cross = jnp.zeros((NLOAD, 1), F32)
    coming = take_faces(par, (xa, xb, ya, yb)) + (rc[...], None)
    for (at, width), got in zip(SEGS, coming):
        seg = slice(at, at + width)
        x = z[:, seg] if got is None else z[:, seg] + got
        image[:, seg] = x
        coef_t += project_rows(x, bh[seg, :], bl[seg, :])
        xw = x * weight(par, at)
        curve += lanesum(q[:, seg] * xw)
        cross += lanesum(u[:, seg] * xw)
    rows = message(coef_t, curve, cross)
    row = lax.broadcasted_iota(jnp.int32, (8, 128), 0)
    modes = jnp.where(row < MODES, rows, 0.0)
    fix_q = jnp.sum(coef_q[48:56] * modes, axis=0, keepdims=True)
    fix_u = jnp.sum(coef_u[48:56] * modes, axis=0, keepdims=True)
    rows = rows - jnp.where(row == 6, fix_q, 0.0) - jnp.where(row == 7, fix_u, 0.0)
    msg[...] = jnp.broadcast_to(rows[None], msg.shape)


def first_image_kernel(z, xa, xb, ya, yb, rc, par, bh, bl, image, msg):
    coef_t = jnp.zeros((NLOAD, 128), F32)
    coming = take_faces(par, (xa, xb, ya, yb)) + (rc[...], None)
    for (at, width), got in zip(SEGS, coming):
        seg = slice(at, at + width)
        x = z[:, seg] if got is None else z[:, seg] + got
        image[:, seg] = x
        coef_t += project_rows(x, bh[seg, :], bl[seg, :])
    msg[...] = jnp.broadcast_to(flip(coef_t)[:8][None], msg.shape)


def next_part(seg, at, codes, m, g, w, act, weight):
    bent = w * w
    if at == CON:
        free = 1.0 - act
        free_grad = free * g
        bent = free * bent
        chopped = act * jnp.minimum(g, 0.0)
        trial = jnp.maximum(m - step_scale * free_grad, 0.0)
    else:
        free_grad = g
        chopped = 0.0
        trial = m - step_scale * g
    u = jnp.where(codes == 0, free_grad, jnp.where(codes == 2, chopped, trial - m))
    return u, lanesum(g * u * weight), lanesum(bent * weight)


def first_update_kernel(
    g, vh, vl, codes, point, image, act, par, t_stack, bh, bl,
    gradient, u, msg,
):
    factor = spread(coarse(vh[...], vl[...], g[...]))
    code = codes[:, 0:1]
    coef_t = jnp.zeros((NLOAD, 128), F32)
    slope = jnp.zeros((NLOAD, 1), F32)
    for at, width in SEGS:
        seg = slice(at, at + width)
        grad = image[:, seg] - mm(factor, t_stack[:, seg])
        gradient[:, seg] = grad
        x, slope_part, _ = next_part(seg, at, code, point[:, seg], grad, grad, act[...], weight(par, at))
        u[:, seg] = x
        slope += slope_part
        coef_t += project_rows(x, bh[seg, :], bl[seg, :])
    rows = message(coef_t, jnp.zeros((NLOAD, 1), F32), slope)
    msg[...] = jnp.broadcast_to(rows[None], msg.shape)


def lengths(k, g, codes_rows, scal):
    sums = jnp.sum(g.reshape(128, 8, 128), axis=0)
    curve, cross = sums[6:7], sums[7:8]
    length = jnp.where(codes_rows[k : k + 1] == 1, -1.0, scal[0:1] / curve)
    return length, curve, cross


def update_kernel(
    k, g, vh, vl, codes, codes_rows, scal, point, gradient, q, image, act, par, t_stack, bh, bl,
    point_out, gradient_out, u, scal_out, msg,
):
    got = g[...]
    length, curve, cross = lengths(k, got, codes_rows, scal)
    scal_out[0:1, :] = length
    scal_out[1:2, :] = curve
    scal_out[2:3, :] = cross
    scal_out[3:8, :] = jnp.zeros((5, 128), F32)
    step = flip(jnp.broadcast_to(length, (8, 128)))[:NLOAD, 0:1]
    factor = spread(coarse(vh[...], vl[...], got))
    code = codes[:, k + 1 : k + 2]
    coef_t = jnp.zeros((NLOAD, 128), F32)
    slope = jnp.zeros((NLOAD, 1), F32)
    bend = jnp.zeros((NLOAD, 1), F32)
    for at, width in SEGS:
        seg = slice(at, at + width)
        w = image[:, seg] - mm(factor, t_stack[:, seg])
        m = point[:, seg] - step * q[:, seg]
        grad = gradient[:, seg] - step * w
        point_out[:, seg] = m
        gradient_out[:, seg] = grad
        x, slope_part, bend_part = next_part(seg, at, code, m, grad, w, act[...], weight(par, at))
        u[:, seg] = x
        slope += slope_part
        bend += bend_part
        coef_t += project_rows(x, bh[seg, :], bl[seg, :])
    msg[...] = jnp.broadcast_to(message(coef_t, bend, slope)[None], msg.shape)


def last_update_kernel(
    k, g, vh, vl, codes_rows, scal, point, gradient, q, image, t_stack, o_s, o_g, o_c,
    point_out, gradient_out,
):
    got = g[...]
    length, _, _ = lengths(k, got, codes_rows, scal)
    step = flip(jnp.broadcast_to(length, (8, 128)))[:NLOAD, 0:1]
    factor = spread(coarse(vh[...], vl[...], got))
    for at, width in SEGS:
        seg = slice(at, at + width)
        w = image[:, seg] - mm(factor, t_stack[:, seg])
        m = point[:, seg] - step * q[:, seg]
        grad = gradient[:, seg] - step * w
        order = {512: o_s, 1536: o_g, 2048: o_c}.get(at)
        if order is not None:
            m = shuffle_back(m, order[...])
            grad = shuffle_back(grad, order[...])
        point_out[:, seg] = m
        gradient_out[:, seg] = grad


VMEM_BYTES = 24 * 2**20


def call(kernel, outs, *operands, flops=0):
    moved = sum(x.size * x.dtype.itemsize for x in operands) + sum(
        o.size * o.dtype.itemsize for o in outs
    )
    return pl.pallas_call(
        kernel,
        out_shape=outs,
        compiler_params=pltpu.CompilerParams(vmem_limit_bytes=VMEM_BYTES),
        cost_estimate=pl.CostEstimate(flops=flops, bytes_accessed=moved, transcendentals=0),
    )(*operands)


def call_product(kernel, outs, *operands):
    return pl.pallas_call(
        kernel,
        out_shape=outs,
        scratch_shapes=[pltpu.VMEM((NLOAD, ORDER), BF16)],
        compiler_params=pltpu.CompilerParams(vmem_limit_bytes=VMEM_BYTES),
        cost_estimate=pl.CostEstimate(
            flops=2 * NLOAD * ORDER * ORDER, bytes_accessed=30 * 2**20, transcendentals=0
        ),
    )(*operands)


def shards(
    schur,
    coarse_basis,
    coarse_inverse,
    coarse_coeff,
    dual_load,
    face_order,
    contact_partner,
    active_flags,
    step_codes,
):
    subs, groups = lax.axis_size("sub"), lax.axis_size("grp")
    count = subs * groups
    quarter = groups // 4
    i, j = lax.axis_index("sub"), lax.axis_index("grp")
    sub_pairs = [(s, s + 1) for s in range(subs - 1)]
    grp_pairs = [(s, s + 1) for s in range(groups - 1) if s + 1 not in (quarter, 3 * quarter)]
    across = [(s, (s + groups // 2) % groups) for s in range(groups)]

    def swaps(pairs, odd):
        chosen = [(a, b) for a, b in pairs if a % 2 == odd]
        return chosen + [(b, a) for a, b in chosen]

    def exchange(xc, xb, xa, yb, ya):
        rc = lax.ppermute(xc, "grp", across)
        ra = lax.ppermute(xa, "sub", swaps(sub_pairs, 0))
        rb = lax.ppermute(xb, "sub", swaps(sub_pairs, 1))
        sb = lax.ppermute(yb, "grp", swaps(grp_pairs, 1))
        sa = lax.ppermute(ya, "grp", swaps(grp_pairs, 0))
        return ra, rb, sa, sb, rc

    def gathered(rows):
        return lax.all_to_all(rows, AXES, 0, 0).reshape(count * 8, 128)

    def half(flag):
        return jnp.where(flag, 0.5, 1.0).astype(F32)

    def wide(value, width=FACE):
        return jnp.full((1, width), value, F32)

    schur_block = schur[0]
    lower_g = (j > 0) & (j != quarter) & (j != 3 * quarter)
    upper_g = (j < groups - 1) & (j != quarter - 1) & (j != 3 * quarter - 1)
    par = jnp.concatenate(
        [
            wide((i % 2 == 0).astype(F32)),
            wide((j % 2 == 0).astype(F32)),
            wide(half(i > 0)),
            wide(half(i < subs - 1)),
            wide(half(lower_g)),
            wide(half(upper_g)),
            jnp.zeros((2, FACE), F32),
        ]
    )
    blocks = coarse_inverse.reshape(MODES, count, MODES)
    vp = jnp.pad(blocks, ((0, 2), (0, 0), (0, 2))).reshape(8, count * 8)
    columns = jnp.pad(blocks.transpose(1, 0, 2), ((0, 0), (0, 2), (NLOAD, 128 - NLOAD - MODES)))
    partner = jnp.where(j >= groups // 2, contact_partner, jnp.arange(CONT, dtype=jnp.int32)[None])

    field = sds((NLOAD, ORDER))
    small = sds((8, 128))
    ready = sds((count, 8, 128))
    buffers = [sds((NLOAD, CONT))] + [sds((NLOAD, FACE))] * 4

    o_s, o_g, o_c, basis, coeff, act, code_columns, code_rows, *faces = call(
        prepare_kernel,
        [sds((FACE, FACE), BF16)] * 2
        + [sds((CONT, CONT), BF16), sds((8, ORDER)), small, sds((NLOAD, CONT))]
        + [sds((NLOAD, 128)), small]
        + [sds((48, CONT))]
        + [sds((32, FACE))] * 4,
        coarse_basis[0], vp, coarse_coeff[0], face_order[0], partner, active_flags[0], step_codes, par,
    )
    t_stack, vh, vl, bh, bl, point, msg = call(
        start_kernel,
        [sds((256, ORDER), BF16)]
        + [sds((48, count * 8), BF16)] * 2
        + [sds((ORDER, 128), BF16)] * 2
        + [field, ready],
        basis, vp, coeff, par, columns, schur_block, dual_load[0], *exchange(*faces),
    )
    orders = (o_s, o_g, o_c)

    got = gathered(msg)
    gh, gl, z, *faces = call_product(
        first_search_kernel,
        [sds((16, count * 8), BF16)] * 2 + [field] + buffers,
        got, vh, vl, par, point, t_stack, *orders, dual_load[0], schur_block,
    )
    image, msg = call(first_image_kernel, [field, ready], z, *exchange(*faces), par, bh, bl)
    got = gathered(msg)
    gradient, u, msg = call(
        first_update_kernel,
        [field, field, ready],
        got, vh, vl, code_columns, point, image, act, par, t_stack, bh, bl,
    )
    q = u
    scal = jnp.zeros((8, 128), F32)
    coef_q = jnp.zeros((56, 128), F32)
    for k in range(ITERS):
        got = gathered(msg)
        coef_u, coef_q, scal, q, z, *faces = call_product(
            functools.partial(search_kernel, k),
            [sds((56, 128))] * 2 + [small, field, field] + buffers,
            got, vh, vl, gh, gl, code_rows, scal, coef_q, par, u, q, t_stack, *orders, schur_block,
        )
        image, msg = call(
            image_kernel,
            [field, ready],
            z, *exchange(*faces), par, q, u, coef_u, coef_q, bh, bl,
        )
        got = gathered(msg)
        if k < ITERS - 1:
            point, gradient, u, scal, msg = call(
                functools.partial(update_kernel, k),
                [field, field, field, small, ready],
                got, vh, vl, code_columns, code_rows, scal, point, gradient, q, image, act, par,
                t_stack, bh, bl,
            )
        else:
            point, gradient = call(
                functools.partial(last_update_kernel, k),
                [field, field],
                got, vh, vl, code_rows, scal, point, gradient, q, image, t_stack, *orders,
            )
    return (point[None], gradient[None])


def solution(mesh):
    in_specs = (
        P(AXES, None, None),
        P(AXES, None, None),
        P(AXES, None),
        P(AXES, None, None),
        P(AXES, None, None),
        P(AXES, None, None),
        P(AXES, None),
        P(AXES, None, None),
        P(),
    )
    out_specs = (P(AXES, None, None), P(AXES, None, None))
    return jax.shard_map(shards, mesh=mesh, in_specs=in_specs, out_specs=out_specs, check_vma=False)
```

```python
import functools

import jax
import jax.numpy as jnp
from jax import lax
from jax.experimental import pallas as pl
from jax.experimental.pallas import tpu as pltpu
from jax.sharding import PartitionSpec as P

FACE = 512
CONT = 256
ORDER = 2560
MODES = 6
NLOAD = 96
ITERS = 3
CON = 4 * FACE
SEGS = ((0, 512), (512, 512), (1024, 512), (1536, 512), (2048, 256), (2304, 256))

F32 = jnp.float32
BF16 = jnp.bfloat16
step_scale = 0.2
AXES = ("sub", "grp")


def sds(shape, dtype=F32):
    return jax.ShapeDtypeStruct(shape, dtype)


def mm(a, b):
    return jnp.dot(a, b, preferred_element_type=F32)


def split2(x):
    hi = x.astype(BF16)
    return hi, (x - hi.astype(F32)).astype(BF16)


def turned(x, order):
    return lax.dot_general(x, order, (((1,), (1,)), ((), ())), preferred_element_type=F32)


def parts3(x):
    hi = x.astype(BF16)
    rest = x - hi.astype(F32)
    mid = rest.astype(BF16)
    return hi, mid, (rest - mid.astype(F32)).astype(BF16)


def shuffle(x, order):
    return sum(turned(part, order) for part in parts3(x))


def shuffle_back(x, order):
    return sum(mm(part, order) for part in parts3(x))


def flip(x):
    rows = x.shape[0]
    if rows % 128:
        x = jnp.concatenate([x, jnp.zeros((128 - rows % 128, x.shape[1]), F32)], axis=0)
    return x.T


def cut(width):
    return [(at, min(width, ORDER - at)) for at in range(0, ORDER, width)]


def spread(rows):
    hi = rows.astype(BF16).astype(F32)
    stack = jnp.concatenate([hi, hi, rows - hi, jnp.zeros((112, 128), F32)], axis=0)
    return stack.T[:NLOAD].astype(BF16)


def coarse(vh, vl, g):
    gh, gl = split2(g)
    return mm(vh, gh) + mm(vl, gh) + mm(vh, gl)


def project_rows(x, bh, bl):
    xh, xl = split2(x)
    return mm(xh, bh) + mm(xl, bh) + mm(xh, bl)


def lanesum(x):
    return jnp.sum(x, axis=1, keepdims=True)


def message(coef_t, first, second):
    lane = lax.broadcasted_iota(jnp.int32, coef_t.shape, 1)
    full = jnp.where(lane == 6, first, jnp.where(lane == 7, second, coef_t))
    return flip(full)[:8]


def send_faces(par, faces, refs):
    even_i, even_j = par[0:1, :] > 0.5, par[1:2, :] > 0.5
    f0, f1, f2, f3 = faces
    refs[0][...] = jnp.where(even_i, f1, f0)
    refs[1][...] = jnp.where(even_i, f0, f1)
    refs[2][...] = jnp.where(even_j, f3, f2)
    refs[3][...] = jnp.where(even_j, f2, f3)


def take_faces(par, refs):
    even_i, even_j = par[0:1, :] > 0.5, par[1:2, :] > 0.5
    xa, xb, ya, yb = (ref[...] for ref in refs)
    return (
        jnp.where(even_i, xb, xa),
        jnp.where(even_i, xa, xb),
        jnp.where(even_j, yb, ya),
        jnp.where(even_j, ya, yb),
    )


def weight(par, at):
    if at < CON:
        row = 2 + at // FACE
        return par[row : row + 1, :]
    return 0.5 if at == CON else 1.0


def padded(x, rows, columns):
    if x.shape[1] < columns:
        x = jnp.concatenate([x, jnp.zeros((x.shape[0], columns - x.shape[1]), F32)], axis=1)
    if x.shape[0] < rows:
        x = jnp.concatenate([x, jnp.zeros((rows - x.shape[0], columns), F32)], axis=0)
    return x


def prepare_kernel(
    basis, vp, coeff, face_rows, contact_row, codes, par,
    o_s, o_g, o_c, basis_out, coeff_out, code_columns, code_rows, mc, xb, xa, yb, ya,
):
    for row, out in ((face_rows[0:1, :], o_s), (face_rows[1:2, :], o_g), (contact_row[...], o_c)):
        n = row.shape[1]
        out[...] = (lax.broadcasted_iota(jnp.int32, (n, n), 0) == row).astype(F32).astype(BF16)
    rows = padded(basis[...], 8, ORDER)
    parts = [
        rows[:, 0:512],
        shuffle(rows[:, 512:1024], o_s[...]),
        rows[:, 1024:1536],
        shuffle(rows[:, 1536:2048], o_g[...]),
        shuffle(rows[:, 2048:2304], o_c[...]),
        rows[:, 2304:2560],
    ]
    for (at, width), part in zip(SEGS, parts):
        basis_out[:, at : at + width] = part
    code = padded(codes[...].astype(F32), NLOAD, 128)
    code_columns[...] = code
    code_rows[...] = flip(code)[:8]
    inv = vp[...]
    own = padded(coeff[...], 8, 512)
    coeff_out[...] = own[:, :128]
    extra = [inv[:, 0:512], inv[:, 512:1024], own]
    send_faces(
        par,
        [jnp.concatenate([part] + extra, axis=0) for part in parts[:4]],
        (xa, xb, ya, yb),
    )
    mc[0:8, :] = parts[4]
    for k in range(4):
        mc[8 + 8 * k : 16 + 8 * k, :] = inv[:, 256 * k : 256 * k + 256]
    mc[40:48, :] = own[:, :256]


def start_kernel(
    basis, vp, coeff, par, columns, flags, o_c, xa, xb, ya, yb, rc,
    t_stack, vh, vl, bh, bl, act_out, point, msg,
):
    zero8 = jnp.zeros((8, ORDER), F32)
    pieces = [basis[...]]
    rows = [vp[...]]
    coefs = [coeff[...]]
    for k, got in enumerate(take_faces(par, (xa, xb, ya, yb))):
        at = FACE * k
        left = [zero8[:, :at]] if at else []
        pieces.append(jnp.concatenate(left + [got[0:8, :], zero8[:, at + FACE :]], axis=1))
        rows.append(jnp.concatenate([got[8:16, :], got[16:24, :]], axis=1))
        coefs.append(got[24:32, 0:128])
    pieces.append(jnp.concatenate([zero8[:, :CON], rc[0:8, :], zero8[:, CON + CONT :]], axis=1))
    rows.append(jnp.concatenate([rc[8 + 8 * k : 16 + 8 * k, :] for k in range(4)], axis=1))
    coefs.append(rc[40:48, 0:128])
    th, tl = split2(jnp.concatenate(pieces, axis=0))
    t_stack[0:48, :] = th
    t_stack[48:96, :] = tl
    t_stack[96:144, :] = th
    t_stack[144:256, :] = jnp.zeros((112, ORDER), BF16)
    hi, low = split2(jnp.concatenate(rows, axis=0))
    vh[...] = hi
    vl[...] = low
    bhi, blow = split2(flip(basis[...]))
    bh[...] = bhi
    bl[...] = blow
    factor = spread(jnp.concatenate(coefs, axis=0))
    coef_t = jnp.zeros((NLOAD, 128), F32)
    for at, width in SEGS:
        seg = slice(at, at + width)
        x = mm(factor, t_stack[:, seg])
        if at == CON:
            x = jnp.maximum(x, 0.0)
        point[:, seg] = x
        coef_t += project_rows(x, bh[seg, :], bl[seg, :])
    act_out[...] = turned(flags[...].astype(F32).astype(BF16), o_c[...])
    msg[...] = columns[...] + flip(coef_t)[:8][None]


def rounded(x, at, orders):
    x = x.astype(BF16)
    order = dict(zip((512, 1536, 2048), orders)).get(at)
    return x if order is None else mm(x, order[...]).astype(BF16)


def product(p, schur, orders, par, z, xc, xb, xa, yb, ya, load=None):
    faces = {}
    for n in (4, 0, 1, 2, 3):
        seg = slice(FACE * n, FACE * (n + 1))
        x = mm(p[...], schur[:, seg])
        if load is not None:
            x = x - load[:, seg]
        if n == 4:
            x = jnp.concatenate([shuffle(x[:, :CONT], orders[2][...]), x[:, CONT:]], axis=1)
        elif n in (1, 3):
            x = shuffle(x, orders[n // 2][...])
        z[:, seg] = x
    send_faces(par, [z[:, FACE * n : FACE * (n + 1)] for n in range(4)], (xa, xb, ya, yb))
    xc[...] = z[:, CON : CON + CONT]


def first_search_kernel(
    g, vh, vl, par, u, t_stack, o_s, o_g, o_c, load, schur,
    gh, gl, z, xc, xb, xa, yb, ya, p,
):
    orders = (o_s, o_g, o_c)

    column = flip(g[...])[96:112]
    row = lax.broadcasted_iota(jnp.int32, column.shape, 0)
    hi, low = split2(jnp.where(row < MODES, column, 0.0))
    gh[...] = hi
    gl[...] = low
    factor = spread(coarse(vh[...], vl[...], g[...]))
    for at, width in SEGS:
        seg = slice(at, at + width)
        p[:, seg] = rounded(u[:, seg] - mm(factor, t_stack[:, seg]), at, orders)
    product(p, schur, orders, par, z, xc, xb, xa, yb, ya, load)


def search_kernel(
    k, g, vh, vl, gh, gl, codes, scal, prev, par, u, d, t_stack, o_s, o_g, o_c, schur,
    coef_u, coef_q, scal_out, q, z, xc, xb, xa, yb, ya, p,
):
    orders = (o_s, o_g, o_c)

    got = g[...]
    gah, gal = split2(got)
    alpha = mm(vh[...], gah) + mm(vl[...], gah) + mm(vh[...], gal)
    gamma = (mm(gh[...], gah) + mm(gl[...], gah) + mm(gh[...], gal))[:8]
    sums = jnp.sum(got.reshape(128, 8, 128), axis=0)
    mix = jnp.concatenate([alpha, gamma], axis=0)
    coef_u[...] = mix
    scal_out[0:1, :] = sums[7:8]
    scal_out[1:8, :] = jnp.zeros((7, 128), F32)
    if k > 0:
        bend = sums[6:7]
        length, curve, cross = scal[0:1], scal[1:2], scal[2:3]
        both = (codes[k : k + 1] == 0) & (codes[k - 1 : k] == 0)
        factor2 = jnp.where(both, (cross - length * bend) / curve, 0.0)
        mix = jnp.where(factor2 == 0.0, mix, mix - factor2 * prev[...])
        g2 = flip(jnp.broadcast_to(factor2, (8, 128)))[:NLOAD, 0:1]
    coef_q[...] = mix
    factor = spread(mix[:48])
    for at, width in SEGS:
        seg = slice(at, at + width)
        x = u[:, seg]
        if k > 0:
            x = x - g2 * d[:, seg]
        q[:, seg] = x
        p[:, seg] = rounded(x - mm(factor, t_stack[:, seg]), at, orders)

    product(p, schur, orders, par, z, xc, xb, xa, yb, ya)


def image_kernel(
    z, xa, xb, ya, yb, rc, par, q, u, coef_u, coef_q, bh, bl,
    image, msg,
):
    coef_t = jnp.zeros((NLOAD, 128), F32)
    curve = jnp.zeros((NLOAD, 1), F32)
    cross = jnp.zeros((NLOAD, 1), F32)
    coming = take_faces(par, (xa, xb, ya, yb)) + (rc[...], None)
    for (at, width), got in zip(SEGS, coming):
        seg = slice(at, at + width)
        x = z[:, seg] if got is None else z[:, seg] + got
        image[:, seg] = x
        coef_t += project_rows(x, bh[seg, :], bl[seg, :])
        xw = x * weight(par, at)
        curve += lanesum(q[:, seg] * xw)
        cross += lanesum(u[:, seg] * xw)
    rows = message(coef_t, curve, cross)
    row = lax.broadcasted_iota(jnp.int32, (8, 128), 0)
    modes = jnp.where(row < MODES, rows, 0.0)
    fix_q = jnp.sum(coef_q[48:56] * modes, axis=0, keepdims=True)
    fix_u = jnp.sum(coef_u[48:56] * modes, axis=0, keepdims=True)
    rows = rows - jnp.where(row == 6, fix_q, 0.0) - jnp.where(row == 7, fix_u, 0.0)
    msg[...] = jnp.broadcast_to(rows[None], msg.shape)


def first_image_kernel(z, xa, xb, ya, yb, rc, par, bh, bl, image, msg):
    coef_t = jnp.zeros((NLOAD, 128), F32)
    coming = take_faces(par, (xa, xb, ya, yb)) + (rc[...], None)
    for (at, width), got in zip(SEGS, coming):
        seg = slice(at, at + width)
        x = z[:, seg] if got is None else z[:, seg] + got
        image[:, seg] = x
        coef_t += project_rows(x, bh[seg, :], bl[seg, :])
    msg[...] = jnp.broadcast_to(flip(coef_t)[:8][None], msg.shape)


def next_part(seg, at, codes, m, g, w, act, weight):
    bent = w * w
    if at == CON:
        free = 1.0 - act
        free_grad = free * g
        bent = free * bent
        chopped = act * jnp.minimum(g, 0.0)
        trial = jnp.maximum(m - step_scale * free_grad, 0.0)
    else:
        free_grad = g
        chopped = 0.0
        trial = m - step_scale * g
    u = jnp.where(codes == 0, free_grad, jnp.where(codes == 2, chopped, trial - m))
    return u, lanesum(g * u * weight), lanesum(bent * weight)


def first_update_kernel(
    g, vh, vl, codes, point, image, act, par, t_stack, bh, bl,
    gradient, u, msg,
):
    factor = spread(coarse(vh[...], vl[...], g[...]))
    code = codes[:, 0:1]
    coef_t = jnp.zeros((NLOAD, 128), F32)
    slope = jnp.zeros((NLOAD, 1), F32)
    for at, width in SEGS:
        seg = slice(at, at + width)
        grad = image[:, seg] - mm(factor, t_stack[:, seg])
        gradient[:, seg] = grad
        x, slope_part, _ = next_part(seg, at, code, point[:, seg], grad, grad, act[...], weight(par, at))
        u[:, seg] = x
        slope += slope_part
        coef_t += project_rows(x, bh[seg, :], bl[seg, :])
    rows = message(coef_t, jnp.zeros((NLOAD, 1), F32), slope)
    msg[...] = jnp.broadcast_to(rows[None], msg.shape)


def lengths(k, g, codes_rows, scal):
    sums = jnp.sum(g.reshape(128, 8, 128), axis=0)
    curve, cross = sums[6:7], sums[7:8]
    length = jnp.where(codes_rows[k : k + 1] == 1, -1.0, scal[0:1] / curve)
    return length, curve, cross


def update_kernel(
    k, g, vh, vl, codes, codes_rows, scal, point, gradient, q, image, act, par, t_stack, bh, bl,
    point_out, gradient_out, u, scal_out, msg,
):
    got = g[...]
    length, curve, cross = lengths(k, got, codes_rows, scal)
    scal_out[0:1, :] = length
    scal_out[1:2, :] = curve
    scal_out[2:3, :] = cross
    scal_out[3:8, :] = jnp.zeros((5, 128), F32)
    step = flip(jnp.broadcast_to(length, (8, 128)))[:NLOAD, 0:1]
    factor = spread(coarse(vh[...], vl[...], got))
    code = codes[:, k + 1 : k + 2]
    coef_t = jnp.zeros((NLOAD, 128), F32)
    slope = jnp.zeros((NLOAD, 1), F32)
    bend = jnp.zeros((NLOAD, 1), F32)
    for at, width in SEGS:
        seg = slice(at, at + width)
        w = image[:, seg] - mm(factor, t_stack[:, seg])
        m = point[:, seg] - step * q[:, seg]
        grad = gradient[:, seg] - step * w
        point_out[:, seg] = m
        gradient_out[:, seg] = grad
        x, slope_part, bend_part = next_part(seg, at, code, m, grad, w, act[...], weight(par, at))
        u[:, seg] = x
        slope += slope_part
        bend += bend_part
        coef_t += project_rows(x, bh[seg, :], bl[seg, :])
    msg[...] = jnp.broadcast_to(message(coef_t, bend, slope)[None], msg.shape)


def last_update_kernel(
    k, g, vh, vl, codes_rows, scal, point, gradient, q, image, t_stack, o_s, o_g, o_c,
    point_out, gradient_out,
):
    got = g[...]
    length, _, _ = lengths(k, got, codes_rows, scal)
    step = flip(jnp.broadcast_to(length, (8, 128)))[:NLOAD, 0:1]
    factor = spread(coarse(vh[...], vl[...], got))
    for at, width in SEGS:
        seg = slice(at, at + width)
        w = image[:, seg] - mm(factor, t_stack[:, seg])
        m = point[:, seg] - step * q[:, seg]
        grad = gradient[:, seg] - step * w
        order = {512: o_s, 1536: o_g, 2048: o_c}.get(at)
        if order is not None:
            m = shuffle_back(m, order[...])
            grad = shuffle_back(grad, order[...])
        point_out[:, seg] = m
        gradient_out[:, seg] = grad


VMEM_BYTES = 24 * 2**20
FETCH_FLOPS = 2 * 10**10


def call(kernel, outs, *operands, flops=0):
    moved = sum(x.size * x.dtype.itemsize for x in operands) + sum(
        o.size * o.dtype.itemsize for o in outs
    )
    return pl.pallas_call(
        kernel,
        out_shape=outs,
        compiler_params=pltpu.CompilerParams(vmem_limit_bytes=VMEM_BYTES),
        cost_estimate=pl.CostEstimate(flops=flops, bytes_accessed=moved, transcendentals=0),
    )(*operands)


def call_product(kernel, outs, *operands):
    return pl.pallas_call(
        kernel,
        out_shape=outs,
        scratch_shapes=[pltpu.VMEM((NLOAD, ORDER), BF16)],
        compiler_params=pltpu.CompilerParams(vmem_limit_bytes=VMEM_BYTES),
        cost_estimate=pl.CostEstimate(
            flops=2 * NLOAD * ORDER * ORDER, bytes_accessed=30 * 2**20, transcendentals=0
        ),
    )(*operands)


def shards(
    schur,
    coarse_basis,
    coarse_inverse,
    coarse_coeff,
    dual_load,
    face_order,
    contact_partner,
    active_flags,
    step_codes,
):
    subs, groups = lax.axis_size("sub"), lax.axis_size("grp")
    count = subs * groups
    quarter = groups // 4
    i, j = lax.axis_index("sub"), lax.axis_index("grp")
    sub_pairs = [(s, s + 1) for s in range(subs - 1)]
    grp_pairs = [(s, s + 1) for s in range(groups - 1) if s + 1 not in (quarter, 3 * quarter)]
    across = [(s, (s + groups // 2) % groups) for s in range(groups)]

    def swaps(pairs, odd):
        chosen = [(a, b) for a, b in pairs if a % 2 == odd]
        return chosen + [(b, a) for a, b in chosen]

    def exchange(xc, xb, xa, yb, ya):
        rc = lax.ppermute(xc, "grp", across)
        ra = lax.ppermute(xa, "sub", swaps(sub_pairs, 0))
        rb = lax.ppermute(xb, "sub", swaps(sub_pairs, 1))
        sb = lax.ppermute(yb, "grp", swaps(grp_pairs, 1))
        sa = lax.ppermute(ya, "grp", swaps(grp_pairs, 0))
        return ra, rb, sa, sb, rc

    def gathered(rows):
        return lax.all_to_all(rows, AXES, 0, 0).reshape(count * 8, 128)

    def half(flag):
        return jnp.where(flag, 0.5, 1.0).astype(F32)

    def wide(value, width=FACE):
        return jnp.full((1, width), value, F32)

    schur_block = schur[0]
    lower_g = (j > 0) & (j != quarter) & (j != 3 * quarter)
    upper_g = (j < groups - 1) & (j != quarter - 1) & (j != 3 * quarter - 1)
    par = jnp.concatenate(
        [
            wide((i % 2 == 0).astype(F32)),
            wide((j % 2 == 0).astype(F32)),
            wide(half(i > 0)),
            wide(half(i < subs - 1)),
            wide(half(lower_g)),
            wide(half(upper_g)),
            jnp.zeros((2, FACE), F32),
        ]
    )
    blocks = coarse_inverse.reshape(MODES, count, MODES)
    vp = jnp.pad(blocks, ((0, 2), (0, 0), (0, 2))).reshape(8, count * 8)
    columns = jnp.pad(blocks.transpose(1, 0, 2), ((0, 0), (0, 2), (NLOAD, 128 - NLOAD - MODES)))
    partner = jnp.where(j >= groups // 2, contact_partner, jnp.arange(CONT, dtype=jnp.int32)[None])

    field = sds((NLOAD, ORDER))
    small = sds((8, 128))
    ready = sds((count, 8, 128))
    buffers = [sds((NLOAD, CONT))] + [sds((NLOAD, FACE))] * 4

    o_s, o_g, o_c, basis, coeff, code_columns, code_rows, *faces = call(
        prepare_kernel,
        [sds((FACE, FACE), BF16)] * 2
        + [sds((CONT, CONT), BF16), sds((8, ORDER)), small]
        + [sds((NLOAD, 128)), small]
        + [sds((48, CONT))]
        + [sds((32, FACE))] * 4,
        coarse_basis[0], vp, coarse_coeff[0], face_order[0], partner, step_codes, par,
        flops=FETCH_FLOPS,
    )
    t_stack, vh, vl, bh, bl, act, point, msg = call(
        start_kernel,
        [sds((256, ORDER), BF16)]
        + [sds((48, count * 8), BF16)] * 2
        + [sds((ORDER, 128), BF16)] * 2
        + [sds((NLOAD, CONT)), field, ready],
        basis, vp, coeff, par, columns, active_flags[0], o_c, *exchange(*faces),
        flops=FETCH_FLOPS,
    )
    orders = (o_s, o_g, o_c)

    got = gathered(msg)
    gh, gl, z, *faces = call_product(
        first_search_kernel,
        [sds((16, count * 8), BF16)] * 2 + [field] + buffers,
        got, vh, vl, par, point, t_stack, *orders, dual_load[0], schur_block,
    )
    image, msg = call(first_image_kernel, [field, ready], z, *exchange(*faces), par, bh, bl)
    got = gathered(msg)
    gradient, u, msg = call(
        first_update_kernel,
        [field, field, ready],
        got, vh, vl, code_columns, point, image, act, par, t_stack, bh, bl,
    )
    q = u
    scal = jnp.zeros((8, 128), F32)
    coef_q = jnp.zeros((56, 128), F32)
    for k in range(ITERS):
        got = gathered(msg)
        coef_u, coef_q, scal, q, z, *faces = call_product(
            functools.partial(search_kernel, k),
            [sds((56, 128))] * 2 + [small, field, field] + buffers,
            got, vh, vl, gh, gl, code_rows, scal, coef_q, par, u, q, t_stack, *orders, schur_block,
        )
        image, msg = call(
            image_kernel,
            [field, ready],
            z, *exchange(*faces), par, q, u, coef_u, coef_q, bh, bl,
        )
        got = gathered(msg)
        if k < ITERS - 1:
            point, gradient, u, scal, msg = call(
                functools.partial(update_kernel, k),
                [field, field, field, small, ready],
                got, vh, vl, code_columns, code_rows, scal, point, gradient, q, image, act, par,
                t_stack, bh, bl,
            )
        else:
            point, gradient = call(
                functools.partial(last_update_kernel, k),
                [field, field],
                got, vh, vl, code_rows, scal, point, gradient, q, image, t_stack, *orders,
            )
    return (point[None], gradient[None])


def solution(mesh):
    in_specs = (
        P(AXES, None, None),
        P(AXES, None, None),
        P(AXES, None),
        P(AXES, None, None),
        P(AXES, None, None),
        P(AXES, None, None),
        P(AXES, None),
        P(AXES, None, None),
        P(),
    )
    out_specs = (P(AXES, None, None), P(AXES, None, None))
    return jax.shard_map(shards, mesh=mesh, in_specs=in_specs, out_specs=out_specs, check_vma=False)
```

```python
import functools

import jax
import jax.numpy as jnp
from jax import lax
from jax.experimental import pallas as pl
from jax.experimental.pallas import tpu as pltpu
from jax.sharding import PartitionSpec as P

FACE = 512
CONT = 256
ORDER = 2560
MODES = 6
NLOAD = 96
ITERS = 3
CON = 4 * FACE
SEGS = ((0, 512), (512, 512), (1024, 512), (1536, 512), (2048, 256), (2304, 256))

F32 = jnp.float32
BF16 = jnp.bfloat16
step_scale = 0.2
AXES = ("sub", "grp")


def sds(shape, dtype=F32):
    return jax.ShapeDtypeStruct(shape, dtype)


def mm(a, b):
    return jnp.dot(a, b, preferred_element_type=F32)


def split2(x):
    hi = x.astype(BF16)
    return hi, (x - hi.astype(F32)).astype(BF16)


def turned(x, order):
    return lax.dot_general(x, order, (((1,), (1,)), ((), ())), preferred_element_type=F32)


def parts3(x):
    hi = x.astype(BF16)
    rest = x - hi.astype(F32)
    mid = rest.astype(BF16)
    return hi, mid, (rest - mid.astype(F32)).astype(BF16)


def shuffle(x, order):
    return sum(turned(part, order) for part in parts3(x))


def shuffle_back(x, order):
    return sum(mm(part, order) for part in parts3(x))


def flip(x):
    rows = x.shape[0]
    if rows % 128:
        x = jnp.concatenate([x, jnp.zeros((128 - rows % 128, x.shape[1]), F32)], axis=0)
    return x.T


def cut(width):
    return [(at, min(width, ORDER - at)) for at in range(0, ORDER, width)]


def spread(rows):
    hi = rows.astype(BF16).astype(F32)
    stack = jnp.concatenate([hi, hi, rows - hi, jnp.zeros((112, 128), F32)], axis=0)
    return stack.T[:NLOAD].astype(BF16)


def coarse(vh, vl, g):
    gh, gl = split2(g)
    return mm(vh, gh) + mm(vl, gh) + mm(vh, gl)


def project_rows(x, bh, bl):
    xh, xl = split2(x)
    return mm(xh, bh) + mm(xl, bh) + mm(xh, bl)


def lanesum(x):
    return jnp.sum(x, axis=1, keepdims=True)


def message(coef_t, first, second):
    lane = lax.broadcasted_iota(jnp.int32, coef_t.shape, 1)
    full = jnp.where(lane == 6, first, jnp.where(lane == 7, second, coef_t))
    return flip(full)[:8]


def send_faces(par, faces, refs):
    even_i, even_j = par[0:1, :] > 0.5, par[1:2, :] > 0.5
    f0, f1, f2, f3 = faces
    refs[0][...] = jnp.where(even_i, f1, f0)
    refs[1][...] = jnp.where(even_i, f0, f1)
    refs[2][...] = jnp.where(even_j, f3, f2)
    refs[3][...] = jnp.where(even_j, f2, f3)


def take_faces(par, refs):
    even_i, even_j = par[0:1, :] > 0.5, par[1:2, :] > 0.5
    xa, xb, ya, yb = (ref[...] for ref in refs)
    return (
        jnp.where(even_i, xb, xa),
        jnp.where(even_i, xa, xb),
        jnp.where(even_j, yb, ya),
        jnp.where(even_j, ya, yb),
    )


def weight(par, at):
    if at < CON:
        row = 2 + at // FACE
        return par[row : row + 1, :]
    return 0.5 if at == CON else 1.0


def padded(x, rows, columns):
    if x.shape[1] < columns:
        x = jnp.concatenate([x, jnp.zeros((x.shape[0], columns - x.shape[1]), F32)], axis=1)
    if x.shape[0] < rows:
        x = jnp.concatenate([x, jnp.zeros((rows - x.shape[0], columns), F32)], axis=0)
    return x


def prepare_kernel(
    basis, vp, coeff, face_rows, contact_row, codes, par,
    o_s, o_g, o_c, basis_out, coeff_out, code_columns, code_rows, mc, xb, xa, yb, ya,
):
    for row, out in ((face_rows[0:1, :], o_s), (face_rows[1:2, :], o_g), (contact_row[...], o_c)):
        n = row.shape[1]
        out[...] = (lax.broadcasted_iota(jnp.int32, (n, n), 0) == row).astype(F32).astype(BF16)
    rows = padded(basis[...], 8, ORDER)
    parts = [
        rows[:, 0:512],
        shuffle(rows[:, 512:1024], o_s[...]),
        rows[:, 1024:1536],
        shuffle(rows[:, 1536:2048], o_g[...]),
        shuffle(rows[:, 2048:2304], o_c[...]),
        rows[:, 2304:2560],
    ]
    for (at, width), part in zip(SEGS, parts):
        basis_out[:, at : at + width] = part
    code = padded(codes[...].astype(F32), NLOAD, 128)
    code_columns[...] = code
    code_rows[...] = flip(code)[:8]
    inv = vp[...]
    own = padded(coeff[...], 8, 512)
    coeff_out[...] = own[:, :128]
    extra = [inv[:, 0:512], inv[:, 512:1024], own]
    send_faces(
        par,
        [jnp.concatenate([part] + extra, axis=0) for part in parts[:4]],
        (xa, xb, ya, yb),
    )
    mc[0:8, :] = parts[4]
    for k in range(4):
        mc[8 + 8 * k : 16 + 8 * k, :] = inv[:, 256 * k : 256 * k + 256]
    mc[40:48, :] = own[:, :256]


def start_kernel(
    basis, vp, coeff, par, columns, flags, o_c, early_schur, early_load,
    xa, xb, ya, yb, rc,
    t_stack, vh, vl, bh, bl, act_out, point, msg,
):
    del early_schur, early_load
    zero8 = jnp.zeros((8, ORDER), F32)
    pieces = [basis[...]]
    rows = [vp[...]]
    coefs = [coeff[...]]
    for k, got in enumerate(take_faces(par, (xa, xb, ya, yb))):
        at = FACE * k
        left = [zero8[:, :at]] if at else []
        pieces.append(jnp.concatenate(left + [got[0:8, :], zero8[:, at + FACE :]], axis=1))
        rows.append(jnp.concatenate([got[8:16, :], got[16:24, :]], axis=1))
        coefs.append(got[24:32, 0:128])
    pieces.append(jnp.concatenate([zero8[:, :CON], rc[0:8, :], zero8[:, CON + CONT :]], axis=1))
    rows.append(jnp.concatenate([rc[8 + 8 * k : 16 + 8 * k, :] for k in range(4)], axis=1))
    coefs.append(rc[40:48, 0:128])
    th, tl = split2(jnp.concatenate(pieces, axis=0))
    t_stack[0:48, :] = th
    t_stack[48:96, :] = tl
    t_stack[96:144, :] = th
    t_stack[144:256, :] = jnp.zeros((112, ORDER), BF16)
    hi, low = split2(jnp.concatenate(rows, axis=0))
    vh[...] = hi
    vl[...] = low
    bhi, blow = split2(flip(basis[...]))
    bh[...] = bhi
    bl[...] = blow
    factor = spread(jnp.concatenate(coefs, axis=0))
    coef_t = jnp.zeros((NLOAD, 128), F32)
    for at, width in SEGS:
        seg = slice(at, at + width)
        x = mm(factor, t_stack[:, seg])
        if at == CON:
            x = jnp.maximum(x, 0.0)
        point[:, seg] = x
        coef_t += project_rows(x, bh[seg, :], bl[seg, :])
    act_out[...] = turned(flags[...].astype(F32).astype(BF16), o_c[...])
    msg[...] = columns[...] + flip(coef_t)[:8][None]


def rounded(x, at, orders):
    x = x.astype(BF16)
    order = dict(zip((512, 1536, 2048), orders)).get(at)
    return x if order is None else mm(x, order[...]).astype(BF16)


def product(p, schur, orders, par, z, xc, xb, xa, yb, ya, load=None):
    faces = {}
    for n in (4, 0, 1, 2, 3):
        seg = slice(FACE * n, FACE * (n + 1))
        x = mm(p[...], schur[:, seg])
        if load is not None:
            x = x - load[:, seg]
        if n == 4:
            x = jnp.concatenate([shuffle(x[:, :CONT], orders[2][...]), x[:, CONT:]], axis=1)
        elif n in (1, 3):
            x = shuffle(x, orders[n // 2][...])
        z[:, seg] = x
    send_faces(par, [z[:, FACE * n : FACE * (n + 1)] for n in range(4)], (xa, xb, ya, yb))
    xc[...] = z[:, CON : CON + CONT]


def first_search_kernel(
    g, vh, vl, par, u, t_stack, o_s, o_g, o_c, load, schur,
    gh, gl, z, xc, xb, xa, yb, ya, p,
):
    orders = (o_s, o_g, o_c)

    column = flip(g[...])[96:112]
    row = lax.broadcasted_iota(jnp.int32, column.shape, 0)
    hi, low = split2(jnp.where(row < MODES, column, 0.0))
    gh[...] = hi
    gl[...] = low
    factor = spread(coarse(vh[...], vl[...], g[...]))
    for at, width in SEGS:
        seg = slice(at, at + width)
        p[:, seg] = rounded(u[:, seg] - mm(factor, t_stack[:, seg]), at, orders)
    product(p, schur, orders, par, z, xc, xb, xa, yb, ya, load)


def search_kernel(
    k, g, vh, vl, gh, gl, codes, scal, prev, par, u, d, t_stack, o_s, o_g, o_c, schur,
    coef_u, coef_q, scal_out, q, z, xc, xb, xa, yb, ya, p,
):
    orders = (o_s, o_g, o_c)

    got = g[...]
    gah, gal = split2(got)
    alpha = mm(vh[...], gah) + mm(vl[...], gah) + mm(vh[...], gal)
    gamma = (mm(gh[...], gah) + mm(gl[...], gah) + mm(gh[...], gal))[:8]
    sums = jnp.sum(got.reshape(128, 8, 128), axis=0)
    mix = jnp.concatenate([alpha, gamma], axis=0)
    coef_u[...] = mix
    scal_out[0:1, :] = sums[7:8]
    scal_out[1:8, :] = jnp.zeros((7, 128), F32)
    if k > 0:
        bend = sums[6:7]
        length, curve, cross = scal[0:1], scal[1:2], scal[2:3]
        both = (codes[k : k + 1] == 0) & (codes[k - 1 : k] == 0)
        factor2 = jnp.where(both, (cross - length * bend) / curve, 0.0)
        mix = jnp.where(factor2 == 0.0, mix, mix - factor2 * prev[...])
        g2 = flip(jnp.broadcast_to(factor2, (8, 128)))[:NLOAD, 0:1]
    coef_q[...] = mix
    factor = spread(mix[:48])
    for at, width in SEGS:
        seg = slice(at, at + width)
        x = u[:, seg]
        if k > 0:
            x = x - g2 * d[:, seg]
        q[:, seg] = x
        p[:, seg] = rounded(x - mm(factor, t_stack[:, seg]), at, orders)

    product(p, schur, orders, par, z, xc, xb, xa, yb, ya)


def image_kernel(
    z, xa, xb, ya, yb, rc, par, q, u, coef_u, coef_q, bh, bl,
    image, msg,
):
    coef_t = jnp.zeros((NLOAD, 128), F32)
    curve = jnp.zeros((NLOAD, 1), F32)
    cross = jnp.zeros((NLOAD, 1), F32)
    coming = take_faces(par, (xa, xb, ya, yb)) + (rc[...], None)
    for (at, width), got in zip(SEGS, coming):
        seg = slice(at, at + width)
        x = z[:, seg] if got is None else z[:, seg] + got
        image[:, seg] = x
        coef_t += project_rows(x, bh[seg, :], bl[seg, :])
        xw = x * weight(par, at)
        curve += lanesum(q[:, seg] * xw)
        cross += lanesum(u[:, seg] * xw)
    rows = message(coef_t, curve, cross)
    row = lax.broadcasted_iota(jnp.int32, (8, 128), 0)
    modes = jnp.where(row < MODES, rows, 0.0)
    fix_q = jnp.sum(coef_q[48:56] * modes, axis=0, keepdims=True)
    fix_u = jnp.sum(coef_u[48:56] * modes, axis=0, keepdims=True)
    rows = rows - jnp.where(row == 6, fix_q, 0.0) - jnp.where(row == 7, fix_u, 0.0)
    msg[...] = jnp.broadcast_to(rows[None], msg.shape)


def first_image_kernel(z, xa, xb, ya, yb, rc, par, bh, bl, image, msg):
    coef_t = jnp.zeros((NLOAD, 128), F32)
    coming = take_faces(par, (xa, xb, ya, yb)) + (rc[...], None)
    for (at, width), got in zip(SEGS, coming):
        seg = slice(at, at + width)
        x = z[:, seg] if got is None else z[:, seg] + got
        image[:, seg] = x
        coef_t += project_rows(x, bh[seg, :], bl[seg, :])
    msg[...] = jnp.broadcast_to(flip(coef_t)[:8][None], msg.shape)


def next_part(seg, at, codes, m, g, w, act, weight):
    bent = w * w
    if at == CON:
        free = 1.0 - act
        free_grad = free * g
        bent = free * bent
        chopped = act * jnp.minimum(g, 0.0)
        trial = jnp.maximum(m - step_scale * free_grad, 0.0)
    else:
        free_grad = g
        chopped = 0.0
        trial = m - step_scale * g
    u = jnp.where(codes == 0, free_grad, jnp.where(codes == 2, chopped, trial - m))
    return u, lanesum(g * u * weight), lanesum(bent * weight)


def first_update_kernel(
    g, vh, vl, codes, point, image, act, par, t_stack, bh, bl,
    gradient, u, msg,
):
    factor = spread(coarse(vh[...], vl[...], g[...]))
    code = codes[:, 0:1]
    coef_t = jnp.zeros((NLOAD, 128), F32)
    slope = jnp.zeros((NLOAD, 1), F32)
    for at, width in SEGS:
        seg = slice(at, at + width)
        grad = image[:, seg] - mm(factor, t_stack[:, seg])
        gradient[:, seg] = grad
        x, slope_part, _ = next_part(seg, at, code, point[:, seg], grad, grad, act[...], weight(par, at))
        u[:, seg] = x
        slope += slope_part
        coef_t += project_rows(x, bh[seg, :], bl[seg, :])
    rows = message(coef_t, jnp.zeros((NLOAD, 1), F32), slope)
    msg[...] = jnp.broadcast_to(rows[None], msg.shape)


def lengths(k, g, codes_rows, scal):
    sums = jnp.sum(g.reshape(128, 8, 128), axis=0)
    curve, cross = sums[6:7], sums[7:8]
    length = jnp.where(codes_rows[k : k + 1] == 1, -1.0, scal[0:1] / curve)
    return length, curve, cross


def update_kernel(
    k, g, vh, vl, codes, codes_rows, scal, point, gradient, q, image, act, par, t_stack, bh, bl,
    point_out, gradient_out, u, scal_out, msg,
):
    got = g[...]
    length, curve, cross = lengths(k, got, codes_rows, scal)
    scal_out[0:1, :] = length
    scal_out[1:2, :] = curve
    scal_out[2:3, :] = cross
    scal_out[3:8, :] = jnp.zeros((5, 128), F32)
    step = flip(jnp.broadcast_to(length, (8, 128)))[:NLOAD, 0:1]
    factor = spread(coarse(vh[...], vl[...], got))
    code = codes[:, k + 1 : k + 2]
    coef_t = jnp.zeros((NLOAD, 128), F32)
    slope = jnp.zeros((NLOAD, 1), F32)
    bend = jnp.zeros((NLOAD, 1), F32)
    for at, width in SEGS:
        seg = slice(at, at + width)
        w = image[:, seg] - mm(factor, t_stack[:, seg])
        m = point[:, seg] - step * q[:, seg]
        grad = gradient[:, seg] - step * w
        point_out[:, seg] = m
        gradient_out[:, seg] = grad
        x, slope_part, bend_part = next_part(seg, at, code, m, grad, w, act[...], weight(par, at))
        u[:, seg] = x
        slope += slope_part
        bend += bend_part
        coef_t += project_rows(x, bh[seg, :], bl[seg, :])
    msg[...] = jnp.broadcast_to(message(coef_t, bend, slope)[None], msg.shape)


def last_update_kernel(
    k, g, vh, vl, codes_rows, scal, point, gradient, q, image, t_stack, o_s, o_g, o_c,
    point_out, gradient_out,
):
    got = g[...]
    length, _, _ = lengths(k, got, codes_rows, scal)
    step = flip(jnp.broadcast_to(length, (8, 128)))[:NLOAD, 0:1]
    factor = spread(coarse(vh[...], vl[...], got))
    for at, width in SEGS:
        seg = slice(at, at + width)
        w = image[:, seg] - mm(factor, t_stack[:, seg])
        m = point[:, seg] - step * q[:, seg]
        grad = gradient[:, seg] - step * w
        order = {512: o_s, 1536: o_g, 2048: o_c}.get(at)
        if order is not None:
            m = shuffle_back(m, order[...])
            grad = shuffle_back(grad, order[...])
        point_out[:, seg] = m
        gradient_out[:, seg] = grad


VMEM_BYTES = 24 * 2**20
FETCH_FLOPS = 2 * 10**10


def call(kernel, outs, *operands, flops=0):
    moved = sum(x.size * x.dtype.itemsize for x in operands) + sum(
        o.size * o.dtype.itemsize for o in outs
    )
    return pl.pallas_call(
        kernel,
        out_shape=outs,
        compiler_params=pltpu.CompilerParams(vmem_limit_bytes=VMEM_BYTES),
        cost_estimate=pl.CostEstimate(flops=flops, bytes_accessed=moved, transcendentals=0),
    )(*operands)


def call_product(kernel, outs, *operands):
    return pl.pallas_call(
        kernel,
        out_shape=outs,
        scratch_shapes=[pltpu.VMEM((NLOAD, ORDER), BF16)],
        compiler_params=pltpu.CompilerParams(vmem_limit_bytes=VMEM_BYTES),
        cost_estimate=pl.CostEstimate(
            flops=2 * NLOAD * ORDER * ORDER, bytes_accessed=30 * 2**20, transcendentals=0
        ),
    )(*operands)


def shards(
    schur,
    coarse_basis,
    coarse_inverse,
    coarse_coeff,
    dual_load,
    face_order,
    contact_partner,
    active_flags,
    step_codes,
):
    subs, groups = lax.axis_size("sub"), lax.axis_size("grp")
    count = subs * groups
    quarter = groups // 4
    i, j = lax.axis_index("sub"), lax.axis_index("grp")
    sub_pairs = [(s, s + 1) for s in range(subs - 1)]
    grp_pairs = [(s, s + 1) for s in range(groups - 1) if s + 1 not in (quarter, 3 * quarter)]
    across = [(s, (s + groups // 2) % groups) for s in range(groups)]

    def swaps(pairs, odd):
        chosen = [(a, b) for a, b in pairs if a % 2 == odd]
        return chosen + [(b, a) for a, b in chosen]

    def exchange(xc, xb, xa, yb, ya):
        rc = lax.ppermute(xc, "grp", across)
        ra = lax.ppermute(xa, "sub", swaps(sub_pairs, 0))
        rb = lax.ppermute(xb, "sub", swaps(sub_pairs, 1))
        sb = lax.ppermute(yb, "grp", swaps(grp_pairs, 1))
        sa = lax.ppermute(ya, "grp", swaps(grp_pairs, 0))
        return ra, rb, sa, sb, rc

    def gathered(rows):
        return lax.all_to_all(rows, AXES, 0, 0).reshape(count * 8, 128)

    def half(flag):
        return jnp.where(flag, 0.5, 1.0).astype(F32)

    def wide(value, width=FACE):
        return jnp.full((1, width), value, F32)

    schur_block = schur[0]
    lower_g = (j > 0) & (j != quarter) & (j != 3 * quarter)
    upper_g = (j < groups - 1) & (j != quarter - 1) & (j != 3 * quarter - 1)
    par = jnp.concatenate(
        [
            wide((i % 2 == 0).astype(F32)),
            wide((j % 2 == 0).astype(F32)),
            wide(half(i > 0)),
            wide(half(i < subs - 1)),
            wide(half(lower_g)),
            wide(half(upper_g)),
            jnp.zeros((2, FACE), F32),
        ]
    )
    blocks = coarse_inverse.reshape(MODES, count, MODES)
    vp = jnp.pad(blocks, ((0, 2), (0, 0), (0, 2))).reshape(8, count * 8)
    columns = jnp.pad(blocks.transpose(1, 0, 2), ((0, 0), (0, 2), (NLOAD, 128 - NLOAD - MODES)))
    partner = jnp.where(j >= groups // 2, contact_partner, jnp.arange(CONT, dtype=jnp.int32)[None])

    field = sds((NLOAD, ORDER))
    small = sds((8, 128))
    ready = sds((count, 8, 128))
    buffers = [sds((NLOAD, CONT))] + [sds((NLOAD, FACE))] * 4

    o_s, o_g, o_c, basis, coeff, code_columns, code_rows, *faces = call(
        prepare_kernel,
        [sds((FACE, FACE), BF16)] * 2
        + [sds((CONT, CONT), BF16), sds((8, ORDER)), small]
        + [sds((NLOAD, 128)), small]
        + [sds((48, CONT))]
        + [sds((32, FACE))] * 4,
        coarse_basis[0], vp, coarse_coeff[0], face_order[0], partner, step_codes, par,
        flops=FETCH_FLOPS,
    )
    t_stack, vh, vl, bh, bl, act, point, msg = call(
        start_kernel,
        [sds((256, ORDER), BF16)]
        + [sds((48, count * 8), BF16)] * 2
        + [sds((ORDER, 128), BF16)] * 2
        + [sds((NLOAD, CONT)), field, ready],
        basis, vp, coeff, par, columns, active_flags[0], o_c, schur_block, dual_load[0],
        *exchange(*faces),
    )
    orders = (o_s, o_g, o_c)

    got = gathered(msg)
    gh, gl, z, *faces = call_product(
        first_search_kernel,
        [sds((16, count * 8), BF16)] * 2 + [field] + buffers,
        got, vh, vl, par, point, t_stack, *orders, dual_load[0], schur_block,
    )
    image, msg = call(first_image_kernel, [field, ready], z, *exchange(*faces), par, bh, bl)
    got = gathered(msg)
    gradient, u, msg = call(
        first_update_kernel,
        [field, field, ready],
        got, vh, vl, code_columns, point, image, act, par, t_stack, bh, bl,
    )
    q = u
    scal = jnp.zeros((8, 128), F32)
    coef_q = jnp.zeros((56, 128), F32)
    for k in range(ITERS):
        got = gathered(msg)
        coef_u, coef_q, scal, q, z, *faces = call_product(
            functools.partial(search_kernel, k),
            [sds((56, 128))] * 2 + [small, field, field] + buffers,
            got, vh, vl, gh, gl, code_rows, scal, coef_q, par, u, q, t_stack, *orders, schur_block,
        )
        image, msg = call(
            image_kernel,
            [field, ready],
            z, *exchange(*faces), par, q, u, coef_u, coef_q, bh, bl,
        )
        got = gathered(msg)
        if k < ITERS - 1:
            point, gradient, u, scal, msg = call(
                functools.partial(update_kernel, k),
                [field, field, field, small, ready],
                got, vh, vl, code_columns, code_rows, scal, point, gradient, q, image, act, par,
                t_stack, bh, bl,
            )
        else:
            point, gradient = call(
                functools.partial(last_update_kernel, k),
                [field, field],
                got, vh, vl, code_rows, scal, point, gradient, q, image, t_stack, *orders,
            )
    return (point[None], gradient[None])


def solution(mesh):
    in_specs = (
        P(AXES, None, None),
        P(AXES, None, None),
        P(AXES, None),
        P(AXES, None, None),
        P(AXES, None, None),
        P(AXES, None, None),
        P(AXES, None),
        P(AXES, None, None),
        P(),
    )
    out_specs = (P(AXES, None, None), P(AXES, None, None))
    return jax.shard_map(shards, mesh=mesh, in_specs=in_specs, out_specs=out_specs, check_vma=False)
```

```python
import functools

import jax
import jax.numpy as jnp
from jax import lax
from jax.experimental import pallas as pl
from jax.experimental.pallas import tpu as pltpu
from jax.sharding import PartitionSpec as P

FACE = 512
CONT = 256
ORDER = 2560
MODES = 6
NLOAD = 96
ITERS = 3
CON = 4 * FACE
SEGS = ((0, 512), (512, 512), (1024, 512), (1536, 512), (2048, 256), (2304, 256))

F32 = jnp.float32
BF16 = jnp.bfloat16
step_scale = 0.2
AXES = ("sub", "grp")


def sds(shape, dtype=F32):
    return jax.ShapeDtypeStruct(shape, dtype)


def mm(a, b):
    return jnp.dot(a, b, preferred_element_type=F32)


def split2(x):
    hi = x.astype(BF16)
    return hi, (x - hi.astype(F32)).astype(BF16)


def turned(x, order):
    return lax.dot_general(x, order, (((1,), (1,)), ((), ())), preferred_element_type=F32)


def parts3(x):
    hi = x.astype(BF16)
    rest = x - hi.astype(F32)
    mid = rest.astype(BF16)
    return hi, mid, (rest - mid.astype(F32)).astype(BF16)


def shuffle(x, order):
    return sum(turned(part, order) for part in parts3(x))


def shuffle_back(x, order):
    return sum(mm(part, order) for part in parts3(x))


def flip(x):
    rows = x.shape[0]
    if rows % 128:
        x = jnp.concatenate([x, jnp.zeros((128 - rows % 128, x.shape[1]), F32)], axis=0)
    return x.T


def cut(width):
    return [(at, min(width, ORDER - at)) for at in range(0, ORDER, width)]


def spread(rows):
    hi = rows.astype(BF16).astype(F32)
    stack = jnp.concatenate([hi, hi, rows - hi, jnp.zeros((112, 128), F32)], axis=0)
    return stack.T[:NLOAD].astype(BF16)


def coarse(vh, vl, g):
    gh, gl = split2(g)
    return mm(vh, gh) + mm(vl, gh) + mm(vh, gl)


def project_rows(x, bh, bl):
    xh, xl = split2(x)
    return mm(xh, bh) + mm(xl, bh) + mm(xh, bl)


def lanesum(x):
    return jnp.sum(x, axis=1, keepdims=True)


def message(coef_t, first, second):
    lane = lax.broadcasted_iota(jnp.int32, coef_t.shape, 1)
    full = jnp.where(lane == 6, first, jnp.where(lane == 7, second, coef_t))
    return flip(full)[:8]


def send_faces(par, faces, refs):
    even_i, even_j = par[0:1, :] > 0.5, par[1:2, :] > 0.5
    f0, f1, f2, f3 = faces
    refs[0][...] = jnp.where(even_i, f1, f0)
    refs[1][...] = jnp.where(even_i, f0, f1)
    refs[2][...] = jnp.where(even_j, f3, f2)
    refs[3][...] = jnp.where(even_j, f2, f3)


def take_faces(par, refs):
    even_i, even_j = par[0:1, :] > 0.5, par[1:2, :] > 0.5
    xa, xb, ya, yb = (ref[...] for ref in refs)
    return (
        jnp.where(even_i, xb, xa),
        jnp.where(even_i, xa, xb),
        jnp.where(even_j, yb, ya),
        jnp.where(even_j, ya, yb),
    )


def weight(par, at):
    if at < CON:
        row = 2 + at // FACE
        return par[row : row + 1, :]
    return 0.5 if at == CON else 1.0


def padded(x, rows, columns):
    if x.shape[1] < columns:
        x = jnp.concatenate([x, jnp.zeros((x.shape[0], columns - x.shape[1]), F32)], axis=1)
    if x.shape[0] < rows:
        x = jnp.concatenate([x, jnp.zeros((rows - x.shape[0], columns), F32)], axis=0)
    return x


def prepare_kernel(
    basis, vp, coeff, face_rows, contact_row, codes, par,
    o_s, o_g, o_c, basis_out, coeff_out, code_columns, code_rows, mc, xb, xa, yb, ya,
):
    for row, out in ((face_rows[0:1, :], o_s), (face_rows[1:2, :], o_g), (contact_row[...], o_c)):
        n = row.shape[1]
        out[...] = (lax.broadcasted_iota(jnp.int32, (n, n), 0) == row).astype(F32).astype(BF16)
    rows = padded(basis[...], 8, ORDER)
    parts = [
        rows[:, 0:512],
        shuffle(rows[:, 512:1024], o_s[...]),
        rows[:, 1024:1536],
        shuffle(rows[:, 1536:2048], o_g[...]),
        shuffle(rows[:, 2048:2304], o_c[...]),
        rows[:, 2304:2560],
    ]
    for (at, width), part in zip(SEGS, parts):
        basis_out[:, at : at + width] = part
    code = padded(codes[...].astype(F32), NLOAD, 128)
    code_columns[...] = code
    code_rows[...] = flip(code)[:8]
    inv = vp[...]
    own = padded(coeff[...], 8, 512)
    coeff_out[...] = own[:, :128]
    extra = [inv[:, 0:512], inv[:, 512:1024], own]
    send_faces(
        par,
        [jnp.concatenate([part] + extra, axis=0) for part in parts[:4]],
        (xa, xb, ya, yb),
    )
    mc[0:8, :] = parts[4]
    for k in range(4):
        mc[8 + 8 * k : 16 + 8 * k, :] = inv[:, 256 * k : 256 * k + 256]
    mc[40:48, :] = own[:, :256]


def start_kernel(
    basis, vp, coeff, par, columns, flags, o_c, early_schur, early_load,
    xa, xb, ya, yb, rc,
    t_stack, vh, vl, bh, bl, act_out, point, msg,
):
    del early_schur, early_load
    zero8 = jnp.zeros((8, ORDER), F32)
    pieces = [basis[...]]
    rows = [vp[...]]
    coefs = [coeff[...]]
    for k, got in enumerate(take_faces(par, (xa, xb, ya, yb))):
        at = FACE * k
        left = [zero8[:, :at]] if at else []
        pieces.append(jnp.concatenate(left + [got[0:8, :], zero8[:, at + FACE :]], axis=1))
        rows.append(jnp.concatenate([got[8:16, :], got[16:24, :]], axis=1))
        coefs.append(got[24:32, 0:128])
    pieces.append(jnp.concatenate([zero8[:, :CON], rc[0:8, :], zero8[:, CON + CONT :]], axis=1))
    rows.append(jnp.concatenate([rc[8 + 8 * k : 16 + 8 * k, :] for k in range(4)], axis=1))
    coefs.append(rc[40:48, 0:128])
    th, tl = split2(jnp.concatenate(pieces, axis=0))
    t_stack[0:48, :] = th
    t_stack[48:96, :] = tl
    t_stack[96:144, :] = th
    t_stack[144:256, :] = jnp.zeros((112, ORDER), BF16)
    hi, low = split2(jnp.concatenate(rows, axis=0))
    vh[...] = hi
    vl[...] = low
    bhi, blow = split2(flip(basis[...]))
    bh[...] = bhi
    bl[...] = blow
    factor = spread(jnp.concatenate(coefs, axis=0))
    coef_t = jnp.zeros((NLOAD, 128), F32)
    for at, width in SEGS:
        seg = slice(at, at + width)
        x = mm(factor, t_stack[:, seg])
        if at == CON:
            x = jnp.maximum(x, 0.0)
        point[:, seg] = x
        coef_t += project_rows(x, bh[seg, :], bl[seg, :])
    act_out[...] = turned(flags[...].astype(F32).astype(BF16), o_c[...])
    msg[...] = columns[...] + flip(coef_t)[:8][None]


def rounded(x, at, orders):
    x = x.astype(BF16)
    order = dict(zip((512, 1536, 2048), orders)).get(at)
    return x if order is None else mm(x, order[...]).astype(BF16)


def product(p, schur, orders, par, z, xc, xb, xa, yb, ya, load=None):
    faces = {}
    for n in (4, 0, 1, 2, 3):
        seg = slice(FACE * n, FACE * (n + 1))
        x = mm(p[...], schur[:, seg])
        if load is not None:
            x = x - load[:, seg]
        if n == 4:
            x = jnp.concatenate([shuffle(x[:, :CONT], orders[2][...]), x[:, CONT:]], axis=1)
        elif n in (1, 3):
            x = shuffle(x, orders[n // 2][...])
        z[:, seg] = x
    send_faces(par, [z[:, FACE * n : FACE * (n + 1)] for n in range(4)], (xa, xb, ya, yb))
    xc[...] = z[:, CON : CON + CONT]


def first_search_kernel(
    g, vh, vl, par, u, t_stack, o_s, o_g, o_c, load, schur,
    gh, gl, z, xc, xb, xa, yb, ya, p,
):
    orders = (o_s, o_g, o_c)

    column = flip(g[...])[96:112]
    row = lax.broadcasted_iota(jnp.int32, column.shape, 0)
    hi, low = split2(jnp.where(row < MODES, column, 0.0))
    gh[...] = hi
    gl[...] = low
    factor = spread(coarse(vh[...], vl[...], g[...]))
    for at, width in SEGS:
        seg = slice(at, at + width)
        p[:, seg] = rounded(u[:, seg] - mm(factor, t_stack[:, seg]), at, orders)
    product(p, schur, orders, par, z, xc, xb, xa, yb, ya, load)


def search_kernel(
    k, g, vh, vl, gh, gl, codes, scal, prev, par, u, d, t_stack, o_s, o_g, o_c, schur,
    coef_u, coef_q, scal_out, q, z, xc, xb, xa, yb, ya, p,
):
    orders = (o_s, o_g, o_c)

    got = g[...]
    gah, gal = split2(got)
    alpha = mm(vh[...], gah) + mm(vl[...], gah) + mm(vh[...], gal)
    gamma = (mm(gh[...], gah) + mm(gl[...], gah) + mm(gh[...], gal))[:8]
    sums = jnp.sum(got.reshape(128, 8, 128), axis=0)
    mix = jnp.concatenate([alpha, gamma], axis=0)
    coef_u[...] = mix
    scal_out[0:1, :] = sums[7:8]
    scal_out[1:8, :] = jnp.zeros((7, 128), F32)
    if k > 0:
        bend = sums[6:7]
        length, curve, cross = scal[0:1], scal[1:2], scal[2:3]
        both = (codes[k : k + 1] == 0) & (codes[k - 1 : k] == 0)
        factor2 = jnp.where(both, (cross - length * bend) / curve, 0.0)
        mix = jnp.where(factor2 == 0.0, mix, mix - factor2 * prev[...])
        g2 = flip(jnp.broadcast_to(factor2, (8, 128)))[:NLOAD, 0:1]
    coef_q[...] = mix
    factor = spread(mix[:48])
    for at, width in SEGS:
        seg = slice(at, at + width)
        x = u[:, seg]
        if k > 0:
            x = x - g2 * d[:, seg]
        q[:, seg] = x
        p[:, seg] = rounded(x - mm(factor, t_stack[:, seg]), at, orders)

    product(p, schur, orders, par, z, xc, xb, xa, yb, ya)


def image_kernel(
    z, xa, xb, ya, yb, rc, par, q, u, coef_u, coef_q, bh, bl,
    image, msg,
):
    coef_t = jnp.zeros((NLOAD, 128), F32)
    curve = jnp.zeros((NLOAD, 1), F32)
    cross = jnp.zeros((NLOAD, 1), F32)
    coming = take_faces(par, (xa, xb, ya, yb)) + (rc[...], None)
    for (at, width), got in zip(SEGS, coming):
        seg = slice(at, at + width)
        x = z[:, seg] if got is None else z[:, seg] + got
        image[:, seg] = x
        coef_t += project_rows(x, bh[seg, :], bl[seg, :])
        xw = x * weight(par, at)
        curve += lanesum(q[:, seg] * xw)
        cross += lanesum(u[:, seg] * xw)
    rows = message(coef_t, curve, cross)
    row = lax.broadcasted_iota(jnp.int32, (8, 128), 0)
    modes = jnp.where(row < MODES, rows, 0.0)
    fix_q = jnp.sum(coef_q[48:56] * modes, axis=0, keepdims=True)
    fix_u = jnp.sum(coef_u[48:56] * modes, axis=0, keepdims=True)
    rows = rows - jnp.where(row == 6, fix_q, 0.0) - jnp.where(row == 7, fix_u, 0.0)
    msg[...] = jnp.broadcast_to(rows[None], msg.shape)


def first_image_kernel(z, xa, xb, ya, yb, rc, par, bh, bl, image, msg):
    coef_t = jnp.zeros((NLOAD, 128), F32)
    coming = take_faces(par, (xa, xb, ya, yb)) + (rc[...], None)
    for (at, width), got in zip(SEGS, coming):
        seg = slice(at, at + width)
        x = z[:, seg] if got is None else z[:, seg] + got
        image[:, seg] = x
        coef_t += project_rows(x, bh[seg, :], bl[seg, :])
    msg[...] = jnp.broadcast_to(flip(coef_t)[:8][None], msg.shape)


def next_part(seg, at, codes, m, g, w, act, weight):
    bent = w * w
    if at == CON:
        free = 1.0 - act
        free_grad = free * g
        bent = free * bent
        chopped = act * jnp.minimum(g, 0.0)
        trial = jnp.maximum(m - step_scale * free_grad, 0.0)
    else:
        free_grad = g
        chopped = 0.0
        trial = m - step_scale * g
    u = jnp.where(codes == 0, free_grad, jnp.where(codes == 2, chopped, trial - m))
    return u, lanesum(g * u * weight), lanesum(bent * weight)


def first_update_kernel(
    g, vh, vl, codes, point, image, act, par, t_stack, bh, bl,
    gradient, u, msg,
):
    factor = spread(coarse(vh[...], vl[...], g[...]))
    code = codes[:, 0:1]
    coef_t = jnp.zeros((NLOAD, 128), F32)
    slope = jnp.zeros((NLOAD, 1), F32)
    for at, width in SEGS:
        seg = slice(at, at + width)
        grad = image[:, seg] - mm(factor, t_stack[:, seg])
        gradient[:, seg] = grad
        x, slope_part, _ = next_part(seg, at, code, point[:, seg], grad, grad, act[...], weight(par, at))
        u[:, seg] = x
        slope += slope_part
        coef_t += project_rows(x, bh[seg, :], bl[seg, :])
    rows = message(coef_t, jnp.zeros((NLOAD, 1), F32), slope)
    msg[...] = jnp.broadcast_to(rows[None], msg.shape)


def lengths(k, g, codes_rows, scal):
    sums = jnp.sum(g.reshape(128, 8, 128), axis=0)
    curve, cross = sums[6:7], sums[7:8]
    length = jnp.where(codes_rows[k : k + 1] == 1, -1.0, scal[0:1] / curve)
    return length, curve, cross


def update_kernel(
    k, g, vh, vl, codes, codes_rows, scal, point, gradient, q, image, act, par, t_stack, bh, bl,
    point_out, gradient_out, u, scal_out, msg,
):
    got = g[...]
    length, curve, cross = lengths(k, got, codes_rows, scal)
    scal_out[0:1, :] = length
    scal_out[1:2, :] = curve
    scal_out[2:3, :] = cross
    scal_out[3:8, :] = jnp.zeros((5, 128), F32)
    step = flip(jnp.broadcast_to(length, (8, 128)))[:NLOAD, 0:1]
    factor = spread(coarse(vh[...], vl[...], got))
    code = codes[:, k + 1 : k + 2]
    coef_t = jnp.zeros((NLOAD, 128), F32)
    slope = jnp.zeros((NLOAD, 1), F32)
    bend = jnp.zeros((NLOAD, 1), F32)
    for at, width in SEGS:
        seg = slice(at, at + width)
        w = image[:, seg] - mm(factor, t_stack[:, seg])
        m = point[:, seg] - step * q[:, seg]
        grad = gradient[:, seg] - step * w
        point_out[:, seg] = m
        gradient_out[:, seg] = grad
        x, slope_part, bend_part = next_part(seg, at, code, m, grad, w, act[...], weight(par, at))
        u[:, seg] = x
        slope += slope_part
        bend += bend_part
        coef_t += project_rows(x, bh[seg, :], bl[seg, :])
    msg[...] = jnp.broadcast_to(message(coef_t, bend, slope)[None], msg.shape)


def last_update_kernel(
    k, g, vh, vl, codes_rows, scal, point, gradient, q, image, t_stack, o_s, o_g, o_c,
    point_out, gradient_out,
):
    got = g[...]
    length, _, _ = lengths(k, got, codes_rows, scal)
    step = flip(jnp.broadcast_to(length, (8, 128)))[:NLOAD, 0:1]
    factor = spread(coarse(vh[...], vl[...], got))
    for at, width in SEGS:
        seg = slice(at, at + width)
        w = image[:, seg] - mm(factor, t_stack[:, seg])
        m = point[:, seg] - step * q[:, seg]
        grad = gradient[:, seg] - step * w
        order = {512: o_s, 1536: o_g, 2048: o_c}.get(at)
        if order is not None:
            m = shuffle_back(m, order[...])
            grad = shuffle_back(grad, order[...])
        point_out[:, seg] = m
        gradient_out[:, seg] = grad


VMEM_BYTES = 24 * 2**20
FETCH_FLOPS = 4 * 10**9


def call(kernel, outs, *operands, flops=0):
    moved = sum(x.size * x.dtype.itemsize for x in operands) + sum(
        o.size * o.dtype.itemsize for o in outs
    )
    return pl.pallas_call(
        kernel,
        out_shape=outs,
        compiler_params=pltpu.CompilerParams(vmem_limit_bytes=VMEM_BYTES),
        cost_estimate=pl.CostEstimate(flops=flops, bytes_accessed=moved, transcendentals=0),
    )(*operands)


def call_product(kernel, outs, *operands):
    return pl.pallas_call(
        kernel,
        out_shape=outs,
        scratch_shapes=[pltpu.VMEM((NLOAD, ORDER), BF16)],
        compiler_params=pltpu.CompilerParams(vmem_limit_bytes=VMEM_BYTES),
        cost_estimate=pl.CostEstimate(
            flops=2 * NLOAD * ORDER * ORDER, bytes_accessed=30 * 2**20, transcendentals=0
        ),
    )(*operands)


def shards(
    schur,
    coarse_basis,
    coarse_inverse,
    coarse_coeff,
    dual_load,
    face_order,
    contact_partner,
    active_flags,
    step_codes,
):
    subs, groups = lax.axis_size("sub"), lax.axis_size("grp")
    count = subs * groups
    quarter = groups // 4
    i, j = lax.axis_index("sub"), lax.axis_index("grp")
    sub_pairs = [(s, s + 1) for s in range(subs - 1)]
    grp_pairs = [(s, s + 1) for s in range(groups - 1) if s + 1 not in (quarter, 3 * quarter)]
    across = [(s, (s + groups // 2) % groups) for s in range(groups)]

    def swaps(pairs, odd):
        chosen = [(a, b) for a, b in pairs if a % 2 == odd]
        return chosen + [(b, a) for a, b in chosen]

    def exchange(xc, xb, xa, yb, ya):
        rc = lax.ppermute(xc, "grp", across)
        ra = lax.ppermute(xa, "sub", swaps(sub_pairs, 0))
        rb = lax.ppermute(xb, "sub", swaps(sub_pairs, 1))
        sb = lax.ppermute(yb, "grp", swaps(grp_pairs, 1))
        sa = lax.ppermute(ya, "grp", swaps(grp_pairs, 0))
        return ra, rb, sa, sb, rc

    def gathered(rows):
        return lax.all_to_all(rows, AXES, 0, 0).reshape(count * 8, 128)

    def half(flag):
        return jnp.where(flag, 0.5, 1.0).astype(F32)

    def wide(value, width=FACE):
        return jnp.full((1, width), value, F32)

    schur_block = schur[0]
    lower_g = (j > 0) & (j != quarter) & (j != 3 * quarter)
    upper_g = (j < groups - 1) & (j != quarter - 1) & (j != 3 * quarter - 1)
    par = jnp.concatenate(
        [
            wide((i % 2 == 0).astype(F32)),
            wide((j % 2 == 0).astype(F32)),
            wide(half(i > 0)),
            wide(half(i < subs - 1)),
            wide(half(lower_g)),
            wide(half(upper_g)),
            jnp.zeros((2, FACE), F32),
        ]
    )
    blocks = coarse_inverse.reshape(MODES, count, MODES)
    vp = jnp.pad(blocks, ((0, 2), (0, 0), (0, 2))).reshape(8, count * 8)
    columns = jnp.pad(blocks.transpose(1, 0, 2), ((0, 0), (0, 2), (NLOAD, 128 - NLOAD - MODES)))
    partner = jnp.where(j >= groups // 2, contact_partner, jnp.arange(CONT, dtype=jnp.int32)[None])

    field = sds((NLOAD, ORDER))
    small = sds((8, 128))
    ready = sds((count, 8, 128))
    buffers = [sds((NLOAD, CONT))] + [sds((NLOAD, FACE))] * 4

    o_s, o_g, o_c, basis, coeff, code_columns, code_rows, *faces = call(
        prepare_kernel,
        [sds((FACE, FACE), BF16)] * 2
        + [sds((CONT, CONT), BF16), sds((8, ORDER)), small]
        + [sds((NLOAD, 128)), small]
        + [sds((48, CONT))]
        + [sds((32, FACE))] * 4,
        coarse_basis[0], vp, coarse_coeff[0], face_order[0], partner, step_codes, par,
        flops=FETCH_FLOPS,
    )
    t_stack, vh, vl, bh, bl, act, point, msg = call(
        start_kernel,
        [sds((256, ORDER), BF16)]
        + [sds((48, count * 8), BF16)] * 2
        + [sds((ORDER, 128), BF16)] * 2
        + [sds((NLOAD, CONT)), field, ready],
        basis, vp, coeff, par, columns, active_flags[0], o_c, schur_block, dual_load[0],
        *exchange(*faces),
    )
    orders = (o_s, o_g, o_c)

    got = gathered(msg)
    gh, gl, z, *faces = call_product(
        first_search_kernel,
        [sds((16, count * 8), BF16)] * 2 + [field] + buffers,
        got, vh, vl, par, point, t_stack, *orders, dual_load[0], schur_block,
    )
    image, msg = call(first_image_kernel, [field, ready], z, *exchange(*faces), par, bh, bl)
    got = gathered(msg)
    gradient, u, msg = call(
        first_update_kernel,
        [field, field, ready],
        got, vh, vl, code_columns, point, image, act, par, t_stack, bh, bl,
    )
    q = u
    scal = jnp.zeros((8, 128), F32)
    coef_q = jnp.zeros((56, 128), F32)
    for k in range(ITERS):
        got = gathered(msg)
        coef_u, coef_q, scal, q, z, *faces = call_product(
            functools.partial(search_kernel, k),
            [sds((56, 128))] * 2 + [small, field, field] + buffers,
            got, vh, vl, gh, gl, code_rows, scal, coef_q, par, u, q, t_stack, *orders, schur_block,
        )
        image, msg = call(
            image_kernel,
            [field, ready],
            z, *exchange(*faces), par, q, u, coef_u, coef_q, bh, bl,
        )
        got = gathered(msg)
        if k < ITERS - 1:
            point, gradient, u, scal, msg = call(
                functools.partial(update_kernel, k),
                [field, field, field, small, ready],
                got, vh, vl, code_columns, code_rows, scal, point, gradient, q, image, act, par,
                t_stack, bh, bl,
            )
        else:
            point, gradient = call(
                functools.partial(last_update_kernel, k),
                [field, field],
                got, vh, vl, code_rows, scal, point, gradient, q, image, t_stack, *orders,
            )
    return (point[None], gradient[None])


def solution(mesh):
    in_specs = (
        P(AXES, None, None),
        P(AXES, None, None),
        P(AXES, None),
        P(AXES, None, None),
        P(AXES, None, None),
        P(AXES, None, None),
        P(AXES, None),
        P(AXES, None, None),
        P(),
    )
    out_specs = (P(AXES, None, None), P(AXES, None, None))
    return jax.shard_map(shards, mesh=mesh, in_specs=in_specs, out_specs=out_specs, check_vma=False)
```
